256 devices in a mesh: group: 2 (over x_lo), batch: 4 (over x_hi, core), mp: 32 (over z, y).
Axes of the slice: x: 4 (x_hi: 2, x_lo: 2; x = x_hi * 2 + x_lo), y: 4, z: 8, core: 2. Of those that a mesh axis runs over, the one named last changes fastest.
Arguments:
- pol_hidden: bfloat16 [128, 8192], P('batch'), may hold values from -6 to 6
- pol_gain: float32 [8192], replicated, may hold values from 0.1 to 1.9
- pol_head: bfloat16 [8192, 65536], P(None, ('group', 'batch', 'mp')), may hold values from -16 to 16
- cand_ids: int32 [128, 10], replicated, may hold values from 0 to 65535
- ext_hidden: bfloat16 [640, 8192], P('batch'), may hold values from -6 to 6
- ext_gain: float32 [8192], replicated, may hold values from 0.1 to 1.9
- query_w: bfloat16 [8192, 8192], P('batch', ('group', 'mp')), may hold values from -10 to 10
- key_w: bfloat16 [8192, 8192], P('batch', ('group', 'mp')), may hold values from -0.0625 to 0.0625
- value_w: bfloat16 [8192, 8192], P('batch', ('group', 'mp')), may hold values from -0.0625 to 0.0625
- key_cache: bfloat16 [64, 256, 8192], P('batch', None, ('group', 'mp')), may hold values from -10 to 10
- value_cache: bfloat16 [64, 256, 8192], P('batch', None, ('group', 'mp')), may hold values from -6 to 6
- cache_len: int32 [64], P('batch'), may hold values from 64 to 256, as said below
- score_head: float32 [8192], P(('group', 'mp')), may hold values from -4 to 4
- prev_logprob: float32 [64, 10], P('batch'), may hold values from -12 to -0.5
Outputs:
- cand_logprob: float32 [128, 10], P('batch')
- combined: float32 [64, 10], P('batch')
The draws below stay inside these ranges and needn't reach their ends.
Inputs may be any that keep to these rules, and one draw needn't show every extreme that they name: `cache_len`: every prefix has at least 64 valid positions; some prefix has all 256.
All inputs are finite; a program needn't handle non-finite values.
Results may differ from the reference program's by a relative error of at most 0.006.
Values may be sent and summed in bfloat16 or wider, within the bound.
A program may use at most 128 MiB of HBM per device.

```python
import jax
import jax.numpy as jnp
from jax import lax

D = 8192
VOCAB = 65536
HD = 128
CAND = 10
CTX = 256
HEADS = 64
ROWS = 128
PREV = 64
EXT = 640


def policy_common(key):
    row_key, column_key, direction_key, spacing_key = jax.random.split(key, 4)
    chosen_rows = jax.random.permutation(row_key, ROWS)[:3].astype(jnp.int32)
    chosen_columns = jax.random.permutation(column_key, VOCAB)[:6].astype(jnp.int32)
    direction = jnp.clip(jax.random.normal(direction_key, (3, D), jnp.float32), -3.0, 3.0)
    spacing = jax.random.uniform(spacing_key, (3,), jnp.float32, 1.5, 2.5)
    return (chosen_rows, chosen_columns, direction, spacing)


def reward_common(key):
    prefix_key, candidate_key, position_key, direction_key, pattern_key, spacing_key = jax.random.split(key, 6)
    prefixes = jax.random.permutation(prefix_key, PREV)[:3].astype(jnp.int32)
    candidate_pick = jax.random.randint(candidate_key, (3,), 0, CAND).astype(jnp.int32)
    chosen_rows = prefixes * CAND + candidate_pick
    first_slot = jax.random.randint(position_key, (3,), 0, CTX // 4 - 1).astype(jnp.int32)
    direction = jnp.clip(jax.random.normal(direction_key, (3, D), jnp.float32), -3.0, 3.0)
    pattern = jnp.clip(jax.random.normal(pattern_key, (3, HEADS * HD), jnp.float32), -3.0, 3.0)
    spacing = jax.random.uniform(spacing_key, (3,), jnp.float32, 1.5, 2.5)
    return (prefixes, chosen_rows, first_slot, direction, pattern, spacing)


def draw_pol_hidden(key, part):
    chosen_rows, chosen_columns, direction, spacing = policy_common(key)
    key = jax.random.fold_in(key, 11)
    noise_part = jnp.clip(jax.random.normal(key, (ROWS, D), jnp.float32), -6.0, 6.0)
    return noise_part.at[chosen_rows].set(direction).astype(jnp.bfloat16)


def draw_pol_head(key, part):
    chosen_rows, chosen_columns, direction, spacing = policy_common(key)
    key = jax.random.fold_in(key, 12)
    spread = 3.0 / D ** 0.5
    noise_part = jnp.clip(jax.random.normal(key, (D, VOCAB), jnp.float32), -6.0, 6.0) * spread
    strengths = jnp.array([95.0, 120.0, 150.0], jnp.float32)
    levels = jnp.concatenate([strengths, strengths - spacing]) / D
    aligned = jnp.concatenate([direction, direction], axis=0) * levels[:, None]
    columns_new = noise_part[:, chosen_columns] * 0.1 + aligned.T
    return noise_part.at[:, chosen_columns].set(columns_new).astype(jnp.bfloat16)


def draw_ext_hidden(key, part):
    prefixes, chosen_rows, first_slot, direction, pattern, spacing = reward_common(key)
    key = jax.random.fold_in(key, 13)
    noise_part = jnp.clip(jax.random.normal(key, (EXT, D), jnp.float32), -6.0, 6.0)
    return noise_part.at[chosen_rows].set(direction).astype(jnp.bfloat16)


def draw_query_w(key, part):
    prefixes, chosen_rows, first_slot, direction, pattern, spacing = reward_common(key)
    key = jax.random.fold_in(key, 14)
    noise_part = jnp.clip(jax.random.normal(key, (D, HEADS * HD), jnp.float32), -6.0, 6.0)
    strengths = (100.0, 125.0, 150.0)
    weight_full = noise_part / D ** 0.5
    for member in range(3):
        weight_load = strengths[member] / (3.0 * D * HD ** 0.5)
        weight_full = weight_full + weight_load * direction[member][:, None] * pattern[member][None, :]
    return weight_full.astype(jnp.bfloat16)


def draw_key_cache(key, part):
    prefixes, chosen_rows, first_slot, direction, pattern, spacing = reward_common(key)
    key = jax.random.fold_in(key, 15)
    noise_part = jnp.clip(jax.random.normal(key, (PREV, CTX, HEADS * HD), jnp.float32), -6.0, 6.0)
    strengths = jnp.array([100.0, 125.0, 150.0], jnp.float32)
    nearest = 3.0 * pattern + 0.02 * noise_part[prefixes, first_slot]
    runner_up = 3.0 * (1.0 - spacing / strengths)[:, None] * pattern + 0.02 * noise_part[prefixes, first_slot + 1]
    filled = noise_part.at[prefixes, first_slot].set(nearest)
    filled = filled.at[prefixes, first_slot + 1].set(runner_up)
    return filled.astype(jnp.bfloat16)


def draw_cache_len(key, part):
    key = jax.random.fold_in(key, 7)
    lengths = jax.random.randint(key, (PREV,), CTX // 4, CTX + 1)
    return lengths.at[0].set(CTX).astype(jnp.int32)


def plant(result, stream_key, smallest, top_value):
    spot = [jax.random.randint(jax.random.fold_in(stream_key, axis), (), 0, length) for axis, length in enumerate(result.shape)]
    main_axis = result.shape.index(max(result.shape))
    neighbour = spot[:main_axis] + [(spot[main_axis] + 1) % result.shape[main_axis]] + spot[main_axis + 1:]
    return result.at[tuple(spot)].set(smallest).at[tuple(neighbour)].set(top_value)


def shard_levels(own_key, extent, cuts, least, top_value):
    level = 1.0
    for position, shards_of in cuts:
        heights = jax.random.uniform(jax.random.fold_in(jax.random.fold_in(own_key, 6), position), (shards_of,), jnp.float32, least / len(cuts), top_value / len(cuts))
        level = level * jnp.repeat(jnp.exp(heights), extent[position] // shards_of).reshape((-1,) + (1,) * (len(extent) - 1 - position))
    return level


def noise(own_key, extent, scale, limit, cuts=(), held_as=jnp.bfloat16):
    values = jax.random.normal(own_key, extent, jnp.float32) * scale
    if len(cuts) > 0:
        values = shard_levels(own_key, extent, cuts, -0.22, 0.18) * values
    return jnp.clip(values, min=-limit, max=limit).astype(held_as)


def setup_inputs(seed: int = 0) -> dict:
    splits = jax.random.split(jax.random.key(seed), 15)
    pol_hidden = draw_pol_hidden(jax.random.fold_in(splits[14], 71), 0)
    pol_gain = jnp.clip(1.0 + 0.18 * jax.random.normal(splits[1], (D,), jnp.float32), 0.1, 1.9)
    pol_head = draw_pol_head(jax.random.fold_in(splits[14], 71), 0)
    cand_ids = plant(jax.random.randint(splits[3], (ROWS, CAND), 0, VOCAB), jax.random.fold_in(splits[3], 1), 0, VOCAB - 1).astype(jnp.int32)
    ext_hidden = draw_ext_hidden(jax.random.fold_in(splits[14], 71), 0)
    ext_gain = jnp.clip(1.0 + 0.18 * jax.random.normal(splits[5], (D,), jnp.float32), 0.1, 1.9)
    query_w = draw_query_w(jax.random.fold_in(splits[14], 71), 0)
    key_w = noise(splits[7], (D, HEADS * HD), D ** -0.5, 0.0625, ((0, 4), (1, 64)))
    value_w = noise(splits[8], (D, HEADS * HD), D ** -0.5, 0.0625, ((0, 4), (1, 64)))
    key_cache = draw_key_cache(jax.random.fold_in(splits[14], 71), 0)
    value_cache = noise(splits[10], (PREV, CTX, HEADS * HD), 1.0, 6.0, ((0, 4), (2, 64)))
    cache_len = draw_cache_len(jax.random.fold_in(splits[14], 71), 0)
    score_head = noise(splits[12], (HEADS * HD,), 0.25, 4.0, ((0, 64),), jnp.float32)
    prev_logprob = jnp.clip(-12.0 + 11.5 * jax.random.uniform(splits[13], (PREV, CAND), jnp.float32) ** shard_levels(splits[13], (PREV, CAND), ((0, 4),), -0.2, 0.2), -12.0, -0.5)
    return {"pol_hidden": pol_hidden, "pol_gain": pol_gain, "pol_head": pol_head, "cand_ids": cand_ids, "ext_hidden": ext_hidden, "ext_gain": ext_gain, "query_w": query_w, "key_w": key_w, "value_w": value_w, "key_cache": key_cache, "value_cache": value_cache, "cache_len": cache_len, "score_head": score_head, "prev_logprob": prev_logprob}


def rms_norm(hidden, gain):
    values = hidden.astype(jnp.float32)
    spread = lax.optimization_barrier(jnp.mean(values * values, axis=-1, keepdims=True))
    return (values * lax.rsqrt(spread + 1e-05) * gain).astype(jnp.bfloat16)

def reference(pol_hidden, pol_gain, pol_head, cand_ids, ext_hidden, ext_gain, query_w, key_w, value_w, key_cache, value_cache, cache_len, score_head, prev_logprob):
    pol_normed = rms_norm(pol_hidden, pol_gain)
    logits = jnp.dot(pol_normed, pol_head, preferred_element_type=jnp.float32)
    top = lax.optimization_barrier(jnp.max(logits, axis=1))
    total = lax.optimization_barrier(jnp.sum(jnp.exp(logits - top[:, None]), axis=1))
    picked = jnp.take_along_axis(logits, cand_ids.astype(jnp.int32), axis=1)
    cand_logprob = picked - top[:, None] - jnp.log(total)[:, None]
    ext_normed = rms_norm(ext_hidden, ext_gain)
    query = jnp.dot(ext_normed, query_w, preferred_element_type=jnp.float32).astype(jnp.bfloat16)
    key_new = jnp.dot(ext_normed, key_w, preferred_element_type=jnp.float32).astype(jnp.bfloat16)
    value_new = jnp.dot(ext_normed, value_w, preferred_element_type=jnp.float32).astype(jnp.bfloat16)
    query = query.reshape(PREV, CAND, HEADS, HD).astype(jnp.float32)
    key_new = key_new.reshape(PREV, CAND, HEADS, HD).astype(jnp.float32)
    value_new = value_new.reshape(PREV, CAND, HEADS, HD).astype(jnp.float32)
    keys = key_cache.reshape(PREV, CTX, HEADS, HD).astype(jnp.float32)
    values = value_cache.reshape(PREV, CTX, HEADS, HD).astype(jnp.float32)
    scale = 1.0 / HD ** 0.5
    scores = jnp.einsum('pchd,pthd->pcht', query, keys) * scale
    valid = (jnp.arange(CTX, dtype=jnp.int32)[None, :] < cache_len[:, None])[:, None, None, :]
    scores = jnp.where(valid, scores, -1e+30)
    own = lax.optimization_barrier(jnp.sum(query * key_new, axis=-1)) * scale
    peak = jnp.maximum(lax.optimization_barrier(jnp.max(scores, axis=-1)), own)
    expo = jnp.where(valid, jnp.exp(scores - peak[..., None]), 0.0)
    own_expo = jnp.exp(own - peak)
    whole = lax.optimization_barrier(jnp.sum(expo, axis=-1)) + own_expo
    weights = (expo / whole[..., None]).astype(jnp.bfloat16).astype(jnp.float32)
    own_weight = (own_expo / whole).astype(jnp.bfloat16).astype(jnp.float32)
    attended = jnp.einsum('pcht,pthd->pchd', weights, values) + own_weight[..., None] * value_new
    reward = lax.optimization_barrier(jnp.sum(attended * score_head.reshape(HEADS, HD), axis=(2, 3)))
    combined = reward + prev_logprob
    return (cand_logprob, combined)
```

```python
import functools

import jax
import jax.numpy as jnp
from jax import lax
from jax.experimental import pallas as pl
from jax.experimental.pallas import tpu as pltpu
from jax.sharding import PartitionSpec as P

MESH = pl.DeviceIdType.MESH
F32 = jnp.float32
BF16 = jnp.bfloat16

D = 8192
HD = 128
CAND = 10
CTX = 256
EROWS = 160
HALF = 80
PROWS = 32
SLICE = 2048
CH = 512
VOC = 256


def kernel(
    ph, pg, phead, ids, eh, eg, qw, kw, vw, kc, vc, clen, sh, prev,
    lp_out, rw_out,
    H, EG, PH, PG, PW, IDS, W, KC, VC, CL, SH, PV,
    XR, SB, OB, XP, ACC, SO, RO, ST, RT, CS, CR, R1, R2, R3,
    lsem, ssem, r_pull, r_sib, r_y, r_z, r_psib, r_pp, r_pn, r_pf, r_so, r_st, r_cr, r_1, r_2, r_3,
):
    g = lax.axis_index("group")
    b = lax.axis_index("batch")
    m = lax.axis_index("mp")
    y, z, h, c = m % 4, m // 4, b // 2, b % 2
    oh = 1 - h

    def dev(dg, dh, y_, z_, c_):
        return (dg, 2 * dh + c_, 4 * z_ + y_)

    sib = dev(g, h, y, z, 1 - c)
    opp = [dev(1 - g, oh, y, z, k) for k in range(2)]
    xp_same = dev(g, oh, y, z, c)
    xp_other = dev(g, oh, y, z, 1 - c)
    ydev = [dev(g, h, (y + k) % 4, z, c) for k in range(4)]
    gydev = [dev(1 - g, h, (y + k) % 4, z, c) for k in range(4)]
    zdev = [dev(g, h, y, (z + k) % 8, c) for k in range(8)]

    def load(src, dst, k):
        cp = pltpu.make_async_copy(src, dst, lsem.at[k])
        cp.start()
        return cp

    l_h = [load(eh.at[pl.ds(HALF * s, HALF)], H.at[pl.ds(HALF * s, HALF)], s) for s in range(2)]
    l_eg = load(eg, EG, 2)

    everyone = [sib, *opp, xp_same, xp_other, *ydev[1:], *gydev, *zdev[1:]]
    barrier = pltpu.get_barrier_semaphore()
    for other in everyone:
        pl.semaphore_signal(barrier, inc=1, device_id=other, device_id_type=MESH)

    sends = []

    def send(src, dst, rsem, target):
        cp = pltpu.make_async_remote_copy(
            src_ref=src, dst_ref=dst, send_sem=ssem.at[len(sends)], recv_sem=rsem,
            device_id=target, device_id_type=MESH,
        )
        cp.start()
        sends.append(cp)

    def got(region, rsem):
        pltpu.make_async_copy(region, region, rsem).wait()

    def row_scale(ref, rows):
        acc = jnp.zeros((16, 512), F32)
        for k in range(D // 512):
            v = ref[rows, pl.ds(512 * k, 512)].astype(F32)
            acc = acc + v * v
        mean = jnp.sum(acc, axis=1, keepdims=True) * (1.0 / D)
        return lax.rsqrt(mean + 1e-05)

    jj = y * (1 - c) + (z % 4) * c

    def norm_piece(ref, gain, rows, r, start, width):
        cols = pl.ds(pl.multiple_of(start, 128), width)
        return (ref[rows, cols].astype(F32) * r * gain[:, cols]).astype(BF16)

    def ext_norm(i, _):
        rows = pl.ds(pl.multiple_of(16 * i, 16), 16)
        r = row_scale(H, rows)
        for k in range(2):
            OB[k, rows, :] = norm_piece(H, EG, rows, r, (2 * oh + k) * SLICE + jj * CH, CH)
        own = pl.ds(pl.multiple_of(EROWS * b + 16 * i, 16), 16)
        for j in range(4):
            SB[j, rows, :] = norm_piece(H, EG, rows, r, (2 * h + 1 - c) * SLICE + j * CH, CH)
            XR[j, own, :] = norm_piece(H, EG, rows, r, b * SLICE + j * CH, CH)
        return 0

    def xr_rows(block, s):
        return pl.ds(pl.multiple_of(EROWS * block + HALF * s, 16), HALF)

    def half(s):
        return pl.ds(HALF * s, HALF)

    l_eg.wait()
    for s in range(2):
        l_h[s].wait()
        if s == 1:
            l_ph = load(ph, PH, 3)
            l_pg = load(pg, PG, 4)
            l_w = [load(w, W.at[:, pl.ds(HD * k, HD)], 5 + k) for k, w in enumerate((qw, kw, vw))]
        lax.fori_loop(5 * s, 5 * s + 5, ext_norm, 0)
        if s == 0:
            pl.semaphore_wait(barrier, len(everyone))
        for k in range(2):
            send(OB.at[k, half(s)], XR.at[jj, xr_rows(b, s)], r_pull.at[c, s], opp[k])
        send(SB.at[:, half(s)], XR.at[:, xr_rows(b, s)], r_sib.at[s], sib)

    l_kc = load(kc, KC, 8)
    l_vc = load(vc, VC, 9)
    l_pw = load(phead, PW, 10)
    l_small = [load(ids, IDS.at[pl.ds(0, CAND)], 11), load(clen, CL, 12), load(sh, SH, 13), load(prev, PV, 14)]

    l_ph.wait()
    l_pg.wait()

    def pol_norm(i, _):
        rows = pl.ds(pl.multiple_of(16 * i, 16), 16)
        own = pl.ds(pl.multiple_of(PROWS * b + 16 * i, 16), 16)
        r = row_scale(PH, rows)
        for j in range(4):
            for k in range(4):
                XP[j, own, pl.ds(CH * k, CH)] = norm_piece(PH, PG, rows, r, j * SLICE + k * CH, CH)
        return 0

    lax.fori_loop(0, 2, pol_norm, 0)

    def xp_rows(block):
        return pl.ds(pl.multiple_of(PROWS * block, 16), PROWS)

    own_p = xp_rows(b)

    def pass_on(s):
        region = XR.at[y, xr_rows(2 * oh, s)]
        got(region, r_pull.at[0, s])
        for k in (1, 3, 2):
            send(region, region, r_y.at[k - 1, s], ydev[k])
        region = XR.at[z % 4, xr_rows(2 * oh + 1, s)]
        got(region, r_pull.at[1, s])
        send(region, region, r_z.at[0, s], zdev[1])
        send(region, region, r_z.at[1, s], zdev[7])
        send(region, region, r_z.at[2, s], zdev[2 if s == 0 else 6])

    pass_on(0)
    send(XP.at[jj, own_p], XP.at[jj, own_p], r_pp, dev(1 - g, oh, y, z, c))
    send(XP.at[:, own_p], XP.at[:, own_p], r_psib, sib)

    for s in range(2):
        got(XR.at[:, xr_rows(2 * h + 1 - c, s)], r_sib.at[s])
    for cp in l_w:
        cp.wait()

    def project(rows):
        total = None
        for j in range(4):
            term = jnp.dot(XR[j, rows, :], W[pl.ds(CH * j, CH), :], preferred_element_type=F32)
            total = term if total is None else total + term
        return total

    def block_rows(block):
        return pl.ds(pl.multiple_of(EROWS * block, 16), EROWS)

    SO[...] = project(block_rows(2 * h + 1 - c))
    send(SO, RO, r_so, sib)
    ACC[...] = project(block_rows(b))

    pass_on(1)

    def arrive(s):
        for k in (1, 3, 2):
            got(XR.at[(y - k + 4) % 4, xr_rows(2 * oh, s)], r_y.at[k - 1, s])
        rows = xr_rows(2 * oh + 1, s)
        got(XR.at[(z + 7) % 4, rows], r_z.at[0, s])
        got(XR.at[(z + 1) % 4, rows], r_z.at[1, s])
        got(XR.at[(z + 2) % 4, rows], r_z.at[2, s])

    def exchange(s):
        arrive(s)
        ST[s] = project(xr_rows(2 * oh + 1 - c, s))
        send(ST.at[s], RT.at[s], r_st.at[s], sib)
        CS[s] = project(xr_rows(2 * oh + c, s))

    def cross(s):
        got(RT.at[s], r_st.at[s])
        CS[s] = CS[s] + RT[s]
        send(CS.at[s], CR.at[s], r_cr.at[s], xp_same)

    exchange(0)
    cross(0)

    pol_src = xp_rows(2 * oh + c)
    region = XP.at[jj, pol_src]
    got(region, r_pp)
    adev = [
        dev(g, h, (y + k * (1 - c)) % 4, (z + k * c) % 8, c) for k in (1, 7, 2, 6)
    ]
    lo = pl.ds(pl.multiple_of(PROWS * (2 * oh + c), 16), 16)
    hi = pl.ds(pl.multiple_of(PROWS * (2 * oh + c) + 16, 16), 16)
    send(region, region, r_pn.at[0], adev[0])
    send(region, region, r_pn.at[1], adev[1])
    send(XP.at[jj, lo], XP.at[jj, lo], r_pn.at[2], adev[2])
    send(XP.at[jj, hi], XP.at[jj, hi], r_pn.at[3], adev[3])
    send(region, region, r_pf.at[0], sib)

    exchange(1)
    cross(1)

    region = XP.at[(jj + 3) % 4, pol_src]
    got(region, r_pn.at[0])
    send(region, region, r_pf.at[1], sib)
    region = XP.at[(jj + 1) % 4, pol_src]
    got(region, r_pn.at[1])
    send(region, region, r_pf.at[2], sib)
    got(XP.at[(jj + 2) % 4, lo], r_pn.at[2])
    got(XP.at[(jj + 2) % 4, hi], r_pn.at[3])
    region = XP.at[(jj + 2) % 4, pol_src]
    send(region, region, r_pf.at[3], sib)

    for cp in l_small:
        cp.wait()
    l_kc.wait()
    l_vc.wait()
    got(RO, r_so)
    scale = 1.0 / HD**0.5
    slot = lax.broadcasted_iota(jnp.int32, (128, HALF), 0)
    src = lax.broadcasted_iota(jnp.int32, (128, HALF), 1)
    spread = jnp.where((src == (slot // 16) * CAND + slot % 16) & (slot % 16 < CAND), 1.0, 0.0).astype(BF16)
    r128 = lax.broadcasted_iota(jnp.int32, (128, 128), 0)
    l128 = lax.broadcasted_iota(jnp.int32, (128, 128), 1)
    position = lax.broadcasted_iota(jnp.int32, (128, CTX), 1)
    lens = jnp.pad(CL[...], ((0, 0), (0, 112)))

    def attend(s):
        got(CR.at[s], r_cr.at[s])
        qkv = (ACC[half(s), :] + RO[half(s), :] + CR[s]).astype(BF16)
        qkv = jnp.dot(spread, qkv, preferred_element_type=F32)
        query, key_new, value_new = qkv[:, :HD], qkv[:, HD : 2 * HD], qkv[:, 2 * HD :]
        own = jnp.sum(query * key_new, axis=1, keepdims=True) * scale
        q16 = query.astype(BF16)
        scores = jnp.concatenate(
            [
                lax.dot_general(
                    q16[16 * p : 16 * p + 16], KC[8 * s + p],
                    (((1,), (1,)), ((), ())), preferred_element_type=F32,
                )
                for p in range(8)
            ],
            axis=0,
        ) * scale
        length = jnp.sum(jnp.where(l128 == r128 // 16 + 8 * s, lens, 0), axis=1, keepdims=True)
        valid = position < length
        scores = jnp.where(valid, scores, -1e30)
        peak = jnp.maximum(jnp.max(scores, axis=1, keepdims=True), own)
        expo = jnp.where(valid, jnp.exp(scores - peak), 0.0)
        own_expo = jnp.exp(own - peak)
        whole = jnp.sum(expo, axis=1, keepdims=True) + own_expo
        weights = (expo / whole).astype(BF16)
        own_weight = (own_expo / whole).astype(BF16).astype(F32)
        attended = jnp.concatenate(
            [
                jnp.dot(weights[16 * p : 16 * p + 16], VC[8 * s + p], preferred_element_type=F32)
                for p in range(8)
            ],
            axis=0,
        )
        attended = attended + own_weight * value_new
        part = jnp.sum(attended * SH[...], axis=1, keepdims=True)
        return jnp.sum(jnp.where(r128 == l128, part, 0.0), axis=0, keepdims=True)

    reward0 = attend(0)

    got(XP.at[:, xp_rows(2 * h + 1 - c)], r_psib)
    sib_jj = y * c + (z % 4) * (1 - c)
    pol_sib = xp_rows(2 * oh + 1 - c)
    for k, shift in enumerate((0, 3, 1, 2)):
        got(XP.at[(sib_jj + shift) % 4, pol_sib], r_pf.at[k])
    l_pw.wait()

    def logits_step(j, total):
        w = PW[pl.ds(pl.multiple_of(SLICE * j, SLICE), SLICE), :]
        return total + jnp.dot(XP[j], w, preferred_element_type=F32)

    logits = lax.fori_loop(0, 4, logits_step, jnp.zeros((128, VOC), F32))
    first_col = ((g * 4 + b) * 32 + m) * VOC
    column = lax.broadcasted_iota(jnp.int32, (128, VOC), 1) + first_col
    peak = jnp.max(logits, axis=1, keepdims=True)
    stats = jnp.where(l128 == 0, peak, 0.0)
    stats = jnp.where(l128 == 1, jnp.sum(jnp.exp(logits - peak), axis=1, keepdims=True), stats)
    wanted = jnp.concatenate([IDS[...]] * 8, axis=0).T
    for k in range(CAND):
        pick = jnp.sum(jnp.where(column == wanted[:, k : k + 1], logits, 0.0), axis=1, keepdims=True)
        stats = jnp.where(l128 == 2 + k, pick, stats)
    R1[b] = stats.T[:16]
    for k, other in enumerate((sib, xp_same, xp_other)):
        send(R1.at[b], R1.at[b], r_1.at[k], other)

    reward1 = attend(1)

    sub16 = lax.broadcasted_iota(jnp.int32, (16, 128), 0)

    def merge(parts):
        top = functools.reduce(jnp.maximum, [t[0:1] for t in parts])
        total = None
        for t in parts:
            factor = jnp.where(sub16 == 1, jnp.exp(t[0:1] - top), 1.0)
            total = t * factor if total is None else total + t * factor
        return jnp.where(sub16 == 0, top, total)

    for k, other in enumerate((2 * h + 1 - c, 2 * oh + c, 2 * oh + 1 - c)):
        got(R1.at[other], r_1.at[k])
    me2 = g * 4 + y
    sub8 = lax.broadcasted_iota(jnp.int32, (8, 128), 0)
    R2[me2, 0:16] = merge([R1[k] for k in range(4)])
    R2[me2, 16:24] = jnp.where(sub8 == 0, reward0, jnp.where(sub8 == 1, reward1, 0.0))
    n = 0
    for k in range(4):
        for dg, devs in ((0, ydev), (1, gydev)):
            if k or dg:
                send(R2.at[me2], R2.at[me2], r_2.at[n], devs[k])
                n += 1
    n = 0
    for k in range(4):
        for dg in range(2):
            if k or dg:
                got(R2.at[(g + dg) % 2 * 4 + (y - k + 4) % 4], r_2.at[n])
                n += 1
    R3[z, 0:16] = merge([R2[k, 0:16] for k in range(8)])
    R3[z, 16:24] = functools.reduce(jnp.add, [R2[k, 16:24] for k in range(8)])
    for k in range(1, 8):
        send(R3.at[z], R3.at[z], r_3.at[k - 1], zdev[k])
    for k in range(1, 8):
        got(R3.at[(z - k + 8) % 8], r_3.at[k - 1])
    final = merge([R3[k, 0:16] for k in range(8)])
    reward = functools.reduce(jnp.add, [R3[k, 16:24] for k in range(8)])

    logprob = final - final[0:1] - jnp.log(final[1:2])
    mine = logprob
    for k in range(1, 4):
        mine = jnp.where(b == k, pltpu.roll(logprob, 128 - PROWS * k, 1), mine)
    lp_out[...] = mine[2 : 2 + CAND, :PROWS]
    both = jnp.where(sub16 < 8, reward[0:1], reward[1:2])
    spread_out = jnp.zeros((16, 128), F32)
    for k in range(8):
        spread_out = jnp.where(sub16 % 8 == k, pltpu.roll(both, (128 - 16 * k) % 128, 1), spread_out)
    rw_out[...] = spread_out[:, :CAND] + PV[...]

    for cp in sends:
        cp.wait_send()


def on_device(
    pol_hidden, pol_gain, pol_head, cand_ids, ext_hidden, ext_gain, query_w, key_w, value_w,
    key_cache, value_cache, cache_len, score_head, prev_logprob,
):
    vm = pltpu.VMEM
    dma = pltpu.SemaphoreType.DMA
    logprob, combined = pl.pallas_call(
        kernel,
        out_shape=(
            jax.ShapeDtypeStruct((CAND, PROWS), F32),
            jax.ShapeDtypeStruct((16, CAND), F32),
        ),
        in_specs=[pl.BlockSpec(memory_space=pl.ANY)] * 14,
        out_specs=(pl.BlockSpec(memory_space=vm), pl.BlockSpec(memory_space=vm)),
        scratch_shapes=[
            vm((EROWS, D), BF16),
            vm((1, D), F32),
            vm((PROWS, D), BF16),
            vm((1, D), F32),
            vm((D, VOC), BF16),
            vm((16, 128), jnp.int32),
            vm((SLICE, 3 * HD), BF16),
            vm((16, CTX, HD), BF16),
            vm((16, CTX, HD), BF16),
            vm((1, 16), jnp.int32),
            vm((1, HD), F32),
            vm((16, CAND), F32),
            vm((4, 4 * EROWS, CH), BF16),
            vm((4, EROWS, CH), BF16),
            vm((2, EROWS, CH), BF16),
            vm((4, 4 * PROWS, SLICE), BF16),
            vm((EROWS, 3 * HD), F32),
            vm((EROWS, 3 * HD), F32),
            vm((EROWS, 3 * HD), F32),
            vm((2, HALF, 3 * HD), F32),
            vm((2, HALF, 3 * HD), F32),
            vm((2, HALF, 3 * HD), F32),
            vm((2, HALF, 3 * HD), F32),
            vm((4, 16, 128), F32),
            vm((8, 24, 128), F32),
            vm((8, 24, 128), F32),
            dma((15,)),
            dma((64,)),
            dma((2, 2)),
            dma((2,)),
            dma((3, 2)),
            dma((3, 2)),
            dma,
            dma,
            dma((4,)),
            dma((4,)),
            dma,
            dma((2,)),
            dma((2,)),
            dma((3,)),
            dma((7,)),
            dma((7,)),
        ],
        compiler_params=pltpu.CompilerParams(
            collective_id=0, has_side_effects=True, vmem_limit_bytes=62 << 20
        ),
        name="candidates",
    )(
        pol_hidden, pol_gain.reshape(1, D), pol_head, cand_ids.T, ext_hidden, ext_gain.reshape(1, D),
        query_w, key_w, value_w, key_cache, value_cache, cache_len.reshape(1, 16),
        score_head.reshape(1, HD), prev_logprob,
    )
    return logprob.T, combined


def solution(mesh):
    placed = (
        P("batch", None),
        P(),
        P(None, ("group", "batch", "mp")),
        P(),
        P("batch", None),
        P(),
        P("batch", ("group", "mp")),
        P("batch", ("group", "mp")),
        P("batch", ("group", "mp")),
        P("batch", None, ("group", "mp")),
        P("batch", None, ("group", "mp")),
        P("batch"),
        P(("group", "mp")),
        P("batch", None),
    )
    return jax.shard_map(
        on_device,
        mesh=mesh,
        in_specs=placed,
        out_specs=(P("batch", None), P("batch", None)),
        check_vma=False,
    )
```

```python
import functools

import jax
import jax.numpy as jnp
from jax import lax
from jax.experimental import pallas as pl
from jax.experimental.pallas import tpu as pltpu
from jax.sharding import PartitionSpec as P

MESH = pl.DeviceIdType.MESH
F32 = jnp.float32
BF16 = jnp.bfloat16

D = 8192
HD = 128
CAND = 10
CTX = 256
EROWS = 160
HALF = 80
PROWS = 32
SLICE = 2048
CH = 512
VOC = 256
PART = 32
PARTS = 5


def part(q):
    return pl.ds(PART * q, PART)


def kernel(
    ph, pg, phead, ids, eh, eg, qw, kw, vw, kc, vc, clen, sh, prev,
    out,
    H, EG, PH, PG, PW, IDS, W, KC, VC, CL, SH, PV,
    XR, SB, OB, XP, ACC, SO, RO, ST, RT, CS, CB, CR, R1, Q, S,
    lsem, ssem, r_pull, r_sib, r_y, r_z, r_psib, r_pp, r_pn, r_pf, r_so, r_st, r_cr,
    r_1, r_q, s_q, r_s, s_s, met2, met3,
):
    g = lax.axis_index("group")
    b = lax.axis_index("batch")
    m = lax.axis_index("mp")
    y, z, h, c = m % 4, m // 4, b // 2, b % 2
    oh = 1 - h

    def dev(dg, dh, y_, z_, c_):
        return (dg, 2 * dh + c_, 4 * z_ + y_)

    sib = dev(g, h, y, z, 1 - c)
    opp = [dev(1 - g, oh, y, z, k) for k in range(2)]
    xp_same = dev(g, oh, y, z, c)
    xp_other = dev(g, oh, y, z, 1 - c)
    ydev = [dev(g, h, (y + k) % 4, z, c) for k in range(4)]
    gydev = [dev(1 - g, h, (y + k) % 4, z, c) for k in range(4)]
    zdev = [dev(g, h, y, (z + k) % 8, c) for k in range(8)]

    def load(src, dst, k):
        cp = pltpu.make_async_copy(src, dst, lsem.at[k])
        cp.start()
        return cp

    l_eg = load(eg, EG, 2)
    l_h = [load(eh.at[part(q)], H.at[part(q)], 3 + q) for q in range(PARTS)]
    l_ph = load(ph, PH, 0)
    l_pg = load(pg, PG, 1)

    near = [sib, *opp, xp_same, xp_other, *gydev, *ydev[1:], zdev[1], zdev[2], zdev[6], zdev[7]]
    barrier = pltpu.get_barrier_semaphore()
    for other in near:
        pl.semaphore_signal(barrier, inc=1, device_id=other, device_id_type=MESH)

    sends = []

    def send(src, dst, rsem, target):
        cp = pltpu.make_async_remote_copy(
            src_ref=src, dst_ref=dst, send_sem=ssem.at[len(sends)], recv_sem=rsem,
            device_id=target, device_id_type=MESH,
        )
        cp.start()
        sends.append(cp)

    def got(region, rsem):
        pltpu.make_async_copy(region, region, rsem).wait()

    def row_scale(ref, rows):
        acc = jnp.zeros((16, 512), F32)
        for k in range(D // 512):
            v = ref[rows, pl.ds(512 * k, 512)].astype(F32)
            acc = acc + v * v
        mean = jnp.sum(acc, axis=1, keepdims=True) * (1.0 / D)
        return lax.rsqrt(mean + 1e-05)

    jj = y * (1 - c) + (z % 4) * c

    def norm_piece(ref, gain, rows, r, start, width):
        cols = pl.ds(pl.multiple_of(start, 128), width)
        return (ref[rows, cols].astype(F32) * r * gain[:, cols]).astype(BF16)

    def pol_norm(i, _):
        rows = pl.ds(pl.multiple_of(16 * i, 16), 16)
        own = pl.ds(pl.multiple_of(PROWS * b + 16 * i, 16), 16)
        r = row_scale(PH, rows)
        for j in range(4):
            for k in range(4):
                XP[j, own, pl.ds(CH * k, CH)] = norm_piece(PH, PG, rows, r, j * SLICE + k * CH, CH)
        return 0

    def xp_rows(block):
        return pl.ds(pl.multiple_of(PROWS * block, 16), PROWS)

    def xp_half(block, e):
        return pl.ds(pl.multiple_of(PROWS * block + 16 * e, 16), 16)

    def greet(sem):
        for other in near:
            pl.semaphore_signal(sem, inc=1, device_id=other, device_id_type=MESH)

    def ext_norm(i, _):
        rows = pl.ds(pl.multiple_of(16 * i, 16), 16)
        r = row_scale(H, rows)
        for k in range(2):
            OB[k, rows, :] = norm_piece(H, EG, rows, r, (2 * oh + k) * SLICE + jj * CH, CH)
        own = pl.ds(pl.multiple_of(EROWS * b + 16 * i, 16), 16)
        for j in range(4):
            SB[j, rows, :] = norm_piece(H, EG, rows, r, (2 * h + 1 - c) * SLICE + j * CH, CH)
            XR[j, own, :] = norm_piece(H, EG, rows, r, b * SLICE + j * CH, CH)
        return 0

    def xr_rows(block, q):
        return pl.ds(pl.multiple_of(EROWS * block + PART * q, 16), PART)

    def xr_block(block):
        return pl.ds(pl.multiple_of(EROWS * block, 16), EROWS)

    l_eg.wait()
    for q in range(PARTS):
        l_h[q].wait()
        lax.fori_loop(2 * q, 2 * q + 2, ext_norm, 0)
        if q == 0:
            pl.semaphore_wait(barrier, len(near))
            greet(met2)
        for k in range(2):
            send(OB.at[k, part(q)], XR.at[jj, xr_rows(b, q)], r_pull.at[c, q], opp[k])
    send(SB, XR.at[:, xr_block(b)], r_sib, sib)
    l_w = [load(w, W.at[:, pl.ds(HD * k, HD)], 8 + k) for k, w in enumerate((qw, kw, vw))]

    l_ph.wait()
    l_pg.wait()
    lax.fori_loop(0, 2, pol_norm, 0)
    for e in range(2):
        piece = XP.at[jj, xp_half(b, e)]
        send(piece, piece, r_pp.at[e], dev(1 - g, oh, y, z, c))
    own_p = XP.at[:, xp_rows(b)]
    send(own_p, own_p, r_psib, sib)

    l_pw = load(phead, PW, 11)
    l_kc = load(kc, KC, 12)
    l_vc = load(vc, VC, 13)
    l_small = [
        load(ids, IDS.at[pl.ds(0, CAND)], 14), load(clen, CL, 15), load(sh, SH, 16), load(prev, PV, 17)
    ]

    def project(*pieces):
        total = None
        for j in range(4):
            x = [XR[j, rows, :] for rows in pieces]
            x = x[0] if len(x) == 1 else jnp.concatenate(x, axis=0)
            term = jnp.dot(x, W[pl.ds(CH * j, CH), :], preferred_element_type=F32)
            total = term if total is None else total + term
        return total

    for cp in l_w:
        cp.wait()
    got(XR.at[:, xr_block(2 * h + 1 - c)], r_sib)
    both = project(xr_block(2 * h + 1 - c), xr_block(b))
    SO[...] = both[:EROWS]
    send(SO, RO, r_so, sib)
    ACC[...] = both[EROWS:]

    pl.semaphore_wait(met2, len(near))
    greet(met3)

    pol_src = 2 * oh + c
    adev = [
        dev(g, h, (y + k * (1 - c)) % 4, (z + k * c) % 8, c) for k in (1, 7, 2, 6)
    ]
    def pol_on(e):
        piece = XP.at[jj, xp_half(pol_src, e)]
        got(piece, r_pp.at[e])
        send(piece, piece, r_pn.at[2, e], adev[2 + e])
        send(piece, piece, r_pn.at[0, e], adev[0])
        send(piece, piece, r_pn.at[1, e], adev[1])
        if e == 1:
            piece = XP.at[jj, xp_rows(pol_src)]
            send(piece, piece, r_pf.at[0], sib)

    def pol_pass(k):
        j = (jj + (3, 1, 2)[k]) % 4
        for e in range(2):
            got(XP.at[j, xp_half(pol_src, e)], r_pn.at[k, e])
        piece = XP.at[j, xp_rows(pol_src)]
        send(piece, piece, r_pf.at[k + 1], sib)

    def pass_on(q):
        piece = XR.at[y, xr_rows(2 * oh, q)]
        got(piece, r_pull.at[0, q])
        for k in (2, 1, 3):
            send(piece, piece, r_y.at[k - 1, q], ydev[k])
        piece = XR.at[z % 4, xr_rows(2 * oh + 1, q)]
        got(piece, r_pull.at[1, q])
        send(piece, piece, r_z.at[2, q], zdev[2 if q % 2 == 0 else 6])
        send(piece, piece, r_z.at[0, q], zdev[1])
        send(piece, piece, r_z.at[1, q], zdev[7])

    def exchange(q):
        for k in (1, 3, 2):
            got(XR.at[(y - k + 4) % 4, xr_rows(2 * oh, q)], r_y.at[k - 1, q])
        rows = xr_rows(2 * oh + 1, q)
        got(XR.at[(z + 7) % 4, rows], r_z.at[0, q])
        got(XR.at[(z + 1) % 4, rows], r_z.at[1, q])
        got(XR.at[(z + 2) % 4, rows], r_z.at[2, q])
        both = project(xr_rows(2 * oh + 1 - c, q), xr_rows(2 * oh + c, q))
        ST[q] = both[:PART]
        send(ST.at[q], RT.at[q], r_st.at[q], sib)
        CS[q] = both[PART:]

    def cross(q):
        got(RT.at[q], r_st.at[q])
        total = CS[q] + RT[q]
        query = total[:, :HD]
        high = query.astype(BF16)
        CB[q, :, 0:HD] = high
        CB[q, :, HD : 2 * HD] = (query - high.astype(F32)).astype(BF16)
        CB[q, :, 2 * HD :] = total[:, HD:].astype(BF16)
        send(CB.at[q], CR.at[q], r_cr.at[q], xp_same)

    for q in range(4):
        pass_on(q)
    exchange(0)
    pass_on(4)
    exchange(1)
    cross(0)
    exchange(2)
    cross(1)
    pol_on(0)
    exchange(3)
    cross(2)
    pol_on(1)
    exchange(4)
    cross(3)
    pol_pass(0)
    cross(4)
    pol_pass(1)
    pol_pass(2)
    pl.semaphore_wait(met3, len(near))

    for cp in l_small:
        cp.wait()
    l_kc.wait()
    l_vc.wait()

    scale = 1.0 / HD**0.5
    slot = lax.broadcasted_iota(jnp.int32, (128, HALF), 0)
    src = lax.broadcasted_iota(jnp.int32, (128, HALF), 1)
    spread = jnp.where((src == (slot // 16) * CAND + slot % 16) & (slot % 16 < CAND), 1.0, 0.0).astype(BF16)
    r128 = lax.broadcasted_iota(jnp.int32, (128, 128), 0)
    l128 = lax.broadcasted_iota(jnp.int32, (128, 128), 1)
    position = lax.broadcasted_iota(jnp.int32, (128, CTX), 1)
    lens = jnp.pad(CL[...], ((0, 0), (0, 112)))

    def attend(s):
        if s == 0:
            pieces = [CR[0], CR[1], CR[2, 0:16]]
        else:
            pieces = [CR[2, 16:32], CR[3], CR[4]]
        got_rows = jnp.concatenate(pieces, axis=0).astype(F32)
        got_rows = jnp.concatenate(
            [got_rows[:, :HD] + got_rows[:, HD : 2 * HD], got_rows[:, 2 * HD :]], axis=1
        )
        mine = pl.ds(HALF * s, HALF)
        qkv = (ACC[mine, :] + RO[mine, :] + got_rows).astype(BF16)
        qkv = jnp.dot(spread, qkv, preferred_element_type=F32)
        query, key_new, value_new = qkv[:, :HD], qkv[:, HD : 2 * HD], qkv[:, 2 * HD :]
        own = jnp.sum(query * key_new, axis=1, keepdims=True) * scale
        q16 = query.astype(BF16)
        scores = jnp.concatenate(
            [
                lax.dot_general(
                    q16[16 * p : 16 * p + 16], KC[8 * s + p],
                    (((1,), (1,)), ((), ())), preferred_element_type=F32,
                )
                for p in range(8)
            ],
            axis=0,
        ) * scale
        length = jnp.sum(jnp.where(l128 == r128 // 16 + 8 * s, lens, 0), axis=1, keepdims=True)
        valid = position < length
        scores = jnp.where(valid, scores, -1e30)
        peak = jnp.maximum(jnp.max(scores, axis=1, keepdims=True), own)
        expo = jnp.where(valid, jnp.exp(scores - peak), 0.0)
        own_expo = jnp.exp(own - peak)
        whole = jnp.sum(expo, axis=1, keepdims=True) + own_expo
        weights = (expo / whole).astype(BF16)
        own_weight = (own_expo / whole).astype(BF16).astype(F32)
        attended = jnp.concatenate(
            [
                jnp.dot(weights[16 * p : 16 * p + 16], VC[8 * s + p], preferred_element_type=F32)
                for p in range(8)
            ],
            axis=0,
        )
        attended = attended + own_weight * value_new
        total = jnp.sum(attended * SH[...], axis=1, keepdims=True)
        return jnp.sum(jnp.where(r128 == l128, total, 0.0), axis=0, keepdims=True)

    got(RO, r_so)
    for q in range(3):
        got(CR.at[q], r_cr.at[q])
    reward0 = attend(0)

    got(XP.at[:, xp_rows(2 * h + 1 - c)], r_psib)
    sib_jj = y * c + (z % 4) * (1 - c)
    for k, shift in enumerate((0, 3, 1, 2)):
        got(XP.at[(sib_jj + shift) % 4, xp_rows(2 * oh + 1 - c)], r_pf.at[k])
    l_pw.wait()
    logits = None
    for j in range(4):
        term = jnp.dot(XP[j], PW[pl.ds(SLICE * j, SLICE), :], preferred_element_type=F32)
        logits = term if logits is None else logits + term
    first_col = ((g * 4 + b) * 32 + m) * VOC
    logits = logits.T
    column = lax.broadcasted_iota(jnp.int32, (VOC, 128), 0) + first_col
    wanted = IDS[...]
    peak = jnp.max(logits, axis=0, keepdims=True)
    stats = [peak, jnp.sum(jnp.exp(logits - peak), axis=0, keepdims=True)]
    for k in range(CAND):
        stats.append(jnp.sum(jnp.where(column == wanted[k : k + 1, :], logits, 0.0), axis=0, keepdims=True))
    R1[b] = jnp.concatenate([*stats, jnp.zeros((4, 128), F32)], axis=0)
    for k, other in enumerate((sib, xp_same, xp_other)):
        send(R1.at[b], R1.at[b], r_1.at[k], other)

    me = g * 32 + y * 8 + z

    def spread_far(buf, rsem, sem):
        def far(o):
            return -(o[0] + min(o[1], 4 - o[1]) + min(o[2], 8 - o[2]))

        offsets = [(i, j, k) for i in range(2) for j in range(4) for k in range(8) if i or j or k]
        for i, j, k in sorted(offsets, key=far):
            pltpu.make_async_remote_copy(
                src_ref=buf.at[me], dst_ref=buf.at[me], send_sem=sem, recv_sem=rsem,
                device_id=dev((g + i) % 2, h, (y + j) % 4, (z + k) % 8, c), device_id_type=MESH,
            ).start()

    for q in range(3, PARTS):
        got(CR.at[q], r_cr.at[q])
    reward1 = attend(1)
    Q[me] = jnp.concatenate([reward0, reward1], axis=0)
    spread_far(Q, r_q, s_q)

    sub16 = lax.broadcasted_iota(jnp.int32, (16, 128), 0)

    def merge(parts):
        top = functools.reduce(jnp.maximum, [t[0:1] for t in parts])
        total = None
        for t in parts:
            factor = jnp.where(sub16 == 1, jnp.exp(t[0:1] - top), 1.0)
            total = t * factor if total is None else total + t * factor
        return jnp.where(sub16 == 0, top, total)

    for k, other in enumerate((2 * h + 1 - c, 2 * oh + c, 2 * oh + 1 - c)):
        got(R1.at[other], r_1.at[k])
    total = merge([R1[k] for k in range(4)])
    mine = total
    for k in range(1, 4):
        mine = jnp.where(b == k, pltpu.roll(total, 128 - PROWS * k, 1), mine)
    lane4 = lax.broadcasted_iota(jnp.int32, (4, 128), 1) // PROWS
    packed = jnp.zeros((4, 128), F32)
    for k in range(4):
        rows = jnp.concatenate([mine[4 * r + k : 4 * r + k + 1] for r in range(4)], axis=0)
        packed = jnp.where(lane4 == k, pltpu.roll(rows, PROWS * k, 1) if k else rows, packed)
    S[me] = packed
    spread_far(S, r_s, s_s)

    for cp in sends:
        cp.wait_send()
    others = pl.ds(0, 63)
    got(Q.at[others], r_q)
    reward = jnp.sum(Q[...], axis=0)
    both = jnp.where(sub16 < 8, reward[0:1], reward[1:2])
    spread_out = jnp.zeros((16, 128), F32)
    for k in range(8):
        spread_out = jnp.where(sub16 % 8 == k, pltpu.roll(both, (128 - 16 * k) % 128, 1), spread_out)
    out[16:32, :] = spread_out + jnp.pad(PV[...], ((0, 0), (0, 128 - CAND)))
    got(Q.at[others], s_q)

    got(S.at[others], r_s)
    first = S[:, 0, :]
    lane1 = lax.broadcasted_iota(jnp.int32, (1, 128), 1) // PROWS
    lane64 = lax.broadcasted_iota(jnp.int32, (64, 128), 1) // PROWS
    top = jnp.max(first, axis=0, keepdims=True)
    factor = pltpu.roll(jnp.exp(first - top), PROWS, 1)
    first = jnp.sum(jnp.where(lane64 == 1, first * factor, first), axis=0, keepdims=True)
    total = jnp.sum(S[...], axis=0)
    total = jnp.concatenate([first, total[1:]], axis=0)
    log_total = pltpu.roll(jnp.log(jnp.where(lane1 == 1, first, 1.0)), 128 - PROWS, 1)

    def over_lanes(v):
        v = jnp.where(lane1 == 0, v, 0.0)
        return functools.reduce(jnp.add, [pltpu.roll(v, PROWS * k, 1) if k else v for k in range(4)])

    total = total - over_lanes(top) - over_lanes(log_total)
    for k in range(CAND):
        r, k4 = (k + 2) // 4, (k + 2) % 4
        row = total[r : r + 1]
        out[k : k + 1, :] = pltpu.roll(row, 128 - PROWS * k4, 1) if k4 else row
    got(S.at[others], s_s)


def place(packed, lp_out, rw_out, x, sem):
    cp = pltpu.make_async_copy(packed, x, sem)
    cp.start()
    cp.wait()
    lp_out[...] = x[0:CAND, :PROWS]
    rw_out[...] = x[16:32, :CAND]


def on_device(
    pol_hidden, pol_gain, pol_head, cand_ids, ext_hidden, ext_gain, query_w, key_w, value_w,
    key_cache, value_cache, cache_len, score_head, prev_logprob,
):
    vm = pltpu.VMEM
    dma = pltpu.SemaphoreType.DMA
    packed = pl.pallas_call(
        kernel,
        out_shape=jax.ShapeDtypeStruct((32, 128), F32),
        in_specs=[pl.BlockSpec(memory_space=pl.ANY)] * 14,
        out_specs=pl.BlockSpec(memory_space=vm),
        scratch_shapes=[
            vm((EROWS, D), BF16),
            vm((1, D), F32),
            vm((PROWS, D), BF16),
            vm((1, D), F32),
            vm((D, VOC), BF16),
            vm((16, 128), jnp.int32),
            vm((SLICE, 3 * HD), BF16),
            vm((16, CTX, HD), BF16),
            vm((16, CTX, HD), BF16),
            vm((1, 16), jnp.int32),
            vm((1, HD), F32),
            vm((16, CAND), F32),
            vm((4, 4 * EROWS, CH), BF16),
            vm((4, EROWS, CH), BF16),
            vm((2, EROWS, CH), BF16),
            vm((4, 4 * PROWS, SLICE), BF16),
            vm((EROWS, 3 * HD), F32),
            vm((EROWS, 3 * HD), F32),
            vm((EROWS, 3 * HD), F32),
            vm((PARTS, PART, 3 * HD), F32),
            vm((PARTS, PART, 3 * HD), F32),
            vm((PARTS, PART, 3 * HD), F32),
            vm((PARTS, PART, 4 * HD), BF16),
            vm((PARTS, PART, 4 * HD), BF16),
            vm((4, 16, 128), F32),
            vm((64, 2, 128), F32),
            vm((64, 4, 128), F32),
            dma((18,)),
            dma((128,)),
            dma((2, PARTS)),
            dma,
            dma((3, PARTS)),
            dma((3, PARTS)),
            dma,
            dma((2,)),
            dma((3, 2)),
            dma((4,)),
            dma,
            dma((PARTS,)),
            dma((PARTS,)),
            dma((3,)),
            dma,
            dma,
            dma,
            dma,
            pltpu.SemaphoreType.REGULAR,
            pltpu.SemaphoreType.REGULAR,
        ],
        compiler_params=pltpu.CompilerParams(
            collective_id=0, has_side_effects=True, vmem_limit_bytes=62 << 20
        ),
        name="candidates",
    )(
        pol_hidden, pol_gain.reshape(1, D), pol_head, cand_ids.T, ext_hidden, ext_gain.reshape(1, D),
        query_w, key_w, value_w, key_cache, value_cache, cache_len.reshape(1, 16),
        score_head.reshape(1, HD), prev_logprob,
    )
    logprob, combined = pl.pallas_call(
        place,
        out_shape=(
            jax.ShapeDtypeStruct((CAND, PROWS), F32),
            jax.ShapeDtypeStruct((16, CAND), F32),
        ),
        in_specs=[pl.BlockSpec(memory_space=pl.ANY)],
        scratch_shapes=[vm((32, 128), F32), dma],
        compiler_params=pltpu.CompilerParams(vmem_limit_bytes=62 << 20),
        name="place",
    )(packed)
    return logprob.T, combined


def solution(mesh):
    placed = (
        P("batch", None),
        P(),
        P(None, ("group", "batch", "mp")),
        P(),
        P("batch", None),
        P(),
        P("batch", ("group", "mp")),
        P("batch", ("group", "mp")),
        P("batch", ("group", "mp")),
        P("batch", None, ("group", "mp")),
        P("batch", None, ("group", "mp")),
        P("batch"),
        P(("group", "mp")),
        P("batch", None),
    )
    return jax.shard_map(
        on_device,
        mesh=mesh,
        in_specs=placed,
        out_specs=(P("batch", None), P("batch", None)),
        check_vma=False,
    )
```

```python
import functools

import jax
import jax.numpy as jnp
from jax import lax
from jax.experimental import pallas as pl
from jax.experimental.pallas import tpu as pltpu
from jax.sharding import PartitionSpec as P

MESH = pl.DeviceIdType.MESH
F32 = jnp.float32
BF16 = jnp.bfloat16

D = 8192
HD = 128
CAND = 10
CTX = 256
EROWS = 160
HALF = 80
PROWS = 32
SLICE = 2048
CH = 512
VOC = 256
STARTS = (0, 16, 48, 80, 112, 144)
SIZES = (16, 32, 32, 32, 32, 16)
PARTS = 6
LAST = PARTS - 1


def part(q):
    return pl.ds(STARTS[q], SIZES[q])


def kernel(
    ph, pg, phead, ids, eh, eg, qw, kw, vw, kc, vc, clen, sh, prev,
    out,
    H, EG, PH, PG, PW, IDS, W, KC, VC, CL, SH, PV,
    XR, SB, OB, XP, ACC, SO, RO, ST, RT, CS, CB, CR, CB2, CR2, R1, Q, S,
    lsem, ssem, r_pull, r_sib, r_y, r_z, r_psib, r_pp, r_pn, r_pf, r_so, r_st, r_cr, r_cr2,
    r_1, s_1, r_q, s_q, r_s, s_s, met2, met3, met4,
):
    g = lax.axis_index("group")
    b = lax.axis_index("batch")
    m = lax.axis_index("mp")
    y, z, h, c = m % 4, m // 4, b // 2, b % 2
    oh = 1 - h

    def dev(dg, dh, y_, z_, c_):
        return (dg, 2 * dh + c_, 4 * z_ + y_)

    sib = dev(g, h, y, z, 1 - c)
    opp = [dev(1 - g, oh, y, z, k) for k in range(2)]
    xp_same = dev(g, oh, y, z, c)
    xp_other = dev(g, oh, y, z, 1 - c)
    ydev = [dev(g, h, (y + k) % 4, z, c) for k in range(4)]
    gydev = [dev(1 - g, h, (y + k) % 4, z, c) for k in range(4)]
    zdev = [dev(g, h, y, (z + k) % 8, c) for k in range(8)]

    def load(src, dst, k):
        cp = pltpu.make_async_copy(src, dst, lsem.at[k])
        cp.start()
        return cp

    l_ph = load(ph, PH, 0)
    l_pg = load(pg, PG, 1)
    l_eg = load(eg, EG, 2)
    near = [sib, *opp, gydev[0], ydev[1], ydev[3], zdev[1], zdev[7]]
    near2 = [*near, ydev[2], zdev[2], zdev[6]]
    planes = [*ydev[1:], *gydev]
    barrier = pltpu.get_barrier_semaphore()
    for other in near:
        pl.semaphore_signal(barrier, inc=1, device_id=other, device_id_type=MESH)

    sends = []

    def send(src, dst, rsem, target):
        cp = pltpu.make_async_remote_copy(
            src_ref=src, dst_ref=dst, send_sem=ssem.at[len(sends)], recv_sem=rsem,
            device_id=target, device_id_type=MESH,
        )
        cp.start()
        sends.append(cp)

    def got(region, rsem):
        pltpu.make_async_copy(region, region, rsem).wait()

    def row_scale(ref, rows):
        acc = jnp.zeros((16, 512), F32)
        for k in range(D // 512):
            v = ref[rows, pl.ds(512 * k, 512)].astype(F32)
            acc = acc + v * v
        mean = jnp.sum(acc, axis=1, keepdims=True) * (1.0 / D)
        return lax.rsqrt(mean + 1e-05)

    jj = y * (1 - c) + (z % 4) * c

    def norm_piece(ref, gain, rows, r, start, width):
        cols = pl.ds(pl.multiple_of(start, 128), width)
        return (ref[rows, cols].astype(F32) * r * gain[:, cols]).astype(BF16)

    def pol_norm(i, _):
        rows = pl.ds(pl.multiple_of(16 * i, 16), 16)
        own = pl.ds(pl.multiple_of(PROWS * b + 16 * i, 16), 16)
        r = row_scale(PH, rows)
        for j in range(4):
            for k in range(4):
                XP[j, own, pl.ds(CH * k, CH)] = norm_piece(PH, PG, rows, r, j * SLICE + k * CH, CH)
        return 0

    def xp_rows(block):
        return pl.ds(pl.multiple_of(PROWS * block, 16), PROWS)

    def xp_half(block, e):
        return pl.ds(pl.multiple_of(PROWS * block + 16 * e, 16), 16)

    def greet(sem, others):
        for other in others:
            pl.semaphore_signal(sem, inc=1, device_id=other, device_id_type=MESH)

    l_ph.wait()
    l_pg.wait()
    l_h = [load(eh.at[part(q)], H.at[part(q)], 3 + q) for q in range(PARTS)]
    lax.fori_loop(0, 2, pol_norm, 0)
    pl.semaphore_wait(barrier, len(near))
    greet(met2, near)
    for e in range(2):
        piece = XP.at[jj, xp_half(b, e)]
        send(piece, piece, r_pp.at[e], dev(1 - g, oh, y, z, c))
    own_p = XP.at[:, xp_rows(b)]
    send(own_p, own_p, r_psib, sib)

    def ext_norm(i, _):
        rows = pl.ds(pl.multiple_of(16 * i, 16), 16)
        r = row_scale(H, rows)
        for k in range(2):
            OB[k, rows, :] = norm_piece(H, EG, rows, r, (2 * oh + k) * SLICE + jj * CH, CH)
        own = pl.ds(pl.multiple_of(EROWS * b + 16 * i, 16), 16)
        for j in range(4):
            SB[j, rows, :] = norm_piece(H, EG, rows, r, (2 * h + 1 - c) * SLICE + j * CH, CH)
            XR[j, own, :] = norm_piece(H, EG, rows, r, b * SLICE + j * CH, CH)
        return 0

    def xr_rows(block, q):
        return pl.ds(pl.multiple_of(EROWS * block + STARTS[q], 16), SIZES[q])

    def xr_block(block):
        return pl.ds(pl.multiple_of(EROWS * block, 16), EROWS)

    l_eg.wait()
    def pull(q):
        for k in range(2):
            send(OB.at[k, part(q)], XR.at[jj, xr_rows(b, q)], r_pull.at[c, q], opp[k])

    for q in range(PARTS):
        l_h[q].wait()
        lax.fori_loop(STARTS[q] // 16, (STARTS[q] + SIZES[q]) // 16, ext_norm, 0)
        if q < 2:
            pull(q)
    send(SB, XR.at[:, xr_block(b)], r_sib, sib)
    l_w = [load(w, W.at[:, pl.ds(HD * k, HD)], 9 + k) for k, w in enumerate((qw, kw, vw))]

    l_pw = load(phead, PW, 12)
    l_kc = load(kc, KC, 13)
    l_vc = load(vc, VC, 14)
    l_small = [
        load(ids, IDS.at[pl.ds(0, CAND)], 15), load(clen, CL, 16), load(sh, SH, 17), load(prev, PV, 18)
    ]

    def project(*pieces):
        total = None
        for j in range(4):
            x = [XR[j, rows, :] for rows in pieces]
            x = x[0] if len(x) == 1 else jnp.concatenate(x, axis=0)
            term = jnp.dot(x, W[pl.ds(CH * j, CH), :], preferred_element_type=F32)
            total = term if total is None else total + term
        return total

    for cp in l_w:
        cp.wait()
    got(XR.at[:, xr_block(2 * h + 1 - c)], r_sib)
    both = project(xr_block(2 * h + 1 - c), xr_block(b))
    SO[...] = both[:EROWS]
    send(SO, RO, r_so, sib)
    ACC[...] = both[EROWS:]

    pl.semaphore_wait(met2, len(near))
    greet(met3, near2)

    pol_src = 2 * oh + c
    adev = [
        dev(g, h, (y + k * (1 - c)) % 4, (z + k * c) % 8, c) for k in (1, 7, 2, 6)
    ]
    def pol_on(e):
        piece = XP.at[jj, xp_half(pol_src, e)]
        got(piece, r_pp.at[e])
        send(piece, piece, r_pn.at[2, e], adev[2 + e])
        send(piece, piece, r_pn.at[0, e], adev[0])
        send(piece, piece, r_pn.at[1, e], adev[1])
        if e == 1:
            piece = XP.at[jj, xp_rows(pol_src)]
            send(piece, piece, r_pf.at[0], sib)

    def pol_pass(k):
        j = (jj + (3, 1, 2)[k]) % 4
        for e in range(2):
            got(XP.at[j, xp_half(pol_src, e)], r_pn.at[k, e])
        piece = XP.at[j, xp_rows(pol_src)]
        send(piece, piece, r_pf.at[k + 1], sib)

    def pass_on(q):
        piece = XR.at[y, xr_rows(2 * oh, q)]
        got(piece, r_pull.at[0, q])
        for k in (2, 1, 3):
            send(piece, piece, r_y.at[k - 1, q], ydev[k])
        piece = XR.at[z % 4, xr_rows(2 * oh + 1, q)]
        got(piece, r_pull.at[1, q])
        send(piece, piece, r_z.at[2, q], zdev[2 if q % 2 == 0 else 6])
        send(piece, piece, r_z.at[0, q], zdev[1])
        send(piece, piece, r_z.at[1, q], zdev[7])

    def ready(q):
        for k in (1, 3, 2):
            got(XR.at[(y - k + 4) % 4, xr_rows(2 * oh, q)], r_y.at[k - 1, q])
        rows = xr_rows(2 * oh + 1, q)
        got(XR.at[(z + 7) % 4, rows], r_z.at[0, q])
        got(XR.at[(z + 1) % 4, rows], r_z.at[1, q])
        got(XR.at[(z + 2) % 4, rows], r_z.at[2, q])
        both = project(xr_rows(2 * oh + 1 - c, q), xr_rows(2 * oh + c, q))
        return both[: SIZES[q]], both[SIZES[q] :]

    def exchange(q):
        theirs, ours = ready(q)
        ST[part(q), :] = theirs
        send(ST.at[part(q)], RT.at[part(q)], r_st.at[q], sib)
        CS[part(q), :] = ours

    def split(ref, rows, total):
        query = total[:, :HD]
        high = query.astype(BF16)
        ref[rows, 0:HD] = high
        ref[rows, HD : 2 * HD] = (query - high.astype(F32)).astype(BF16)
        ref[rows, 2 * HD :] = total[:, HD:].astype(BF16)

    def cross(q):
        got(RT.at[part(q)], r_st.at[q])
        split(CB, part(q), CS[part(q), :] + RT[part(q), :])
        send(CB.at[part(q)], CR.at[part(q)], r_cr.at[q], xp_same)

    def cross_last():
        theirs, ours = ready(LAST)
        whole = pl.ds(0, SIZES[LAST])
        split(CB2, whole, theirs)
        send(CB2, CR2, r_cr2, xp_other)
        split(CB, part(LAST), ours)
        send(CB.at[part(LAST)], CR.at[part(LAST)], r_cr.at[LAST], xp_same)

    for cp in l_small:
        cp.wait()

    scale = 1.0 / HD**0.5
    slot = lax.broadcasted_iota(jnp.int32, (128, HALF), 0)
    src = lax.broadcasted_iota(jnp.int32, (128, HALF), 1)
    spread = jnp.where((src == (slot // 16) * CAND + slot % 16) & (slot % 16 < CAND), 1.0, 0.0).astype(BF16)
    r128 = lax.broadcasted_iota(jnp.int32, (128, 128), 0)
    l128 = lax.broadcasted_iota(jnp.int32, (128, 128), 1)
    position = lax.broadcasted_iota(jnp.int32, (128, CTX), 1)
    lens = jnp.pad(CL[...], ((0, 0), (0, 112)))

    def attend(s):
        mine = pl.ds(HALF * s, HALF)
        got_rows = CR[mine, :].astype(F32)
        if s == 1:
            tail = CR2[...].astype(F32)
            got_rows = got_rows + jnp.concatenate([jnp.zeros((HALF - SIZES[LAST], 4 * HD), F32), tail], axis=0)
        got_rows = jnp.concatenate(
            [got_rows[:, :HD] + got_rows[:, HD : 2 * HD], got_rows[:, 2 * HD :]], axis=1
        )
        qkv = (ACC[mine, :] + RO[mine, :] + got_rows).astype(BF16)
        qkv = jnp.dot(spread, qkv, preferred_element_type=F32)
        query, key_new, value_new = qkv[:, :HD], qkv[:, HD : 2 * HD], qkv[:, 2 * HD :]
        own = jnp.sum(query * key_new, axis=1, keepdims=True) * scale
        q16 = query.astype(BF16)
        scores = jnp.concatenate(
            [
                lax.dot_general(
                    q16[16 * p : 16 * p + 16], KC[8 * s + p],
                    (((1,), (1,)), ((), ())), preferred_element_type=F32,
                )
                for p in range(8)
            ],
            axis=0,
        ) * scale
        length = jnp.sum(jnp.where(l128 == r128 // 16 + 8 * s, lens, 0), axis=1, keepdims=True)
        valid = position < length
        scores = jnp.where(valid, scores, -1e30)
        peak = jnp.maximum(jnp.max(scores, axis=1, keepdims=True), own)
        expo = jnp.where(valid, jnp.exp(scores - peak), 0.0)
        own_expo = jnp.exp(own - peak)
        whole = jnp.sum(expo, axis=1, keepdims=True) + own_expo
        weights = (expo / whole).astype(BF16)
        own_weight = (own_expo / whole).astype(BF16).astype(F32)
        attended = jnp.concatenate(
            [
                jnp.dot(weights[16 * p : 16 * p + 16], VC[8 * s + p], preferred_element_type=F32)
                for p in range(8)
            ],
            axis=0,
        )
        attended = attended + own_weight * value_new
        total = jnp.sum(attended * SH[...], axis=1, keepdims=True)
        return jnp.sum(jnp.where(r128 == l128, total, 0.0), axis=0, keepdims=True)

    def spread_one(buf, slot, rsem, sem, target):
        pltpu.make_async_remote_copy(
            src_ref=buf.at[slot], dst_ref=buf.at[slot], send_sem=sem, recv_sem=rsem,
            device_id=target, device_id_type=MESH,
        ).start()

    def spread_far(buf, slot, groups, rsem, sem):
        def far(o):
            return -(o[0] + min(o[1], 4 - o[1]) + min(o[2], 8 - o[2]))

        offsets = [(i, j, k) for i in range(groups) for j in range(4) for k in range(8) if i or j or k]
        for i, j, k in sorted(offsets, key=far):
            spread_one(buf, slot, rsem, sem, dev((g + i) % 2, h, (y + j) % 4, (z + k) % 8, c))

    pol_on(0)
    pol_on(1)
    pull(2)
    pass_on(0)
    pull(3)
    pass_on(1)
    pull(4)
    pl.semaphore_wait(met3, len(near2))
    greet(met4, planes)
    pass_on(2)
    pull(5)
    exchange(0)
    pol_pass(0)
    pol_pass(1)
    pass_on(3)
    cross(0)
    pol_pass(2)
    exchange(1)
    pass_on(4)
    pass_on(5)
    got(XP.at[:, xp_rows(2 * h + 1 - c)], r_psib)
    sib_jj = y * c + (z % 4) * (1 - c)
    for k, shift in enumerate((0, 3, 1, 2)):
        got(XP.at[(sib_jj + shift) % 4, xp_rows(2 * oh + 1 - c)], r_pf.at[k])
    l_pw.wait()
    logits = None
    for j in range(4):
        term = jnp.dot(XP[j], PW[pl.ds(SLICE * j, SLICE), :], preferred_element_type=F32)
        logits = term if logits is None else logits + term

    exchange(2)
    cross(1)
    first_col = ((g * 4 + b) * 32 + m) * VOC
    logits = logits.T
    column = lax.broadcasted_iota(jnp.int32, (VOC, 128), 0) + first_col
    wanted = IDS[...]
    peak = jnp.max(logits, axis=0, keepdims=True)
    stats = [peak, jnp.sum(jnp.exp(logits - peak), axis=0, keepdims=True)]
    for k in range(CAND):
        stats.append(jnp.sum(jnp.where(column == wanted[k : k + 1, :], logits, 0.0), axis=0, keepdims=True))
    here = 2 * (2 * h + g) + c
    R1[here] = jnp.concatenate([*stats, jnp.zeros((4, 128), F32)], axis=0)
    for i, j, k in ((1, 0, 0), (1, 0, 1), (1, 1, 0), (1, 1, 1), (0, 1, 0), (0, 1, 1), (0, 0, 1)):
        spread_one(R1, here, r_1, s_1, dev((g + j) % 2, (h + i) % 2, y, z, (c + k) % 2))

    exchange(3)
    cross(2)
    exchange(4)
    cross(3)
    cross_last()
    cross(4)
    pl.semaphore_wait(met4, len(planes))

    sub16 = lax.broadcasted_iota(jnp.int32, (16, 128), 0)

    def merge(parts):
        top = functools.reduce(jnp.maximum, [t[0:1] for t in parts])
        total = None
        for t in parts:
            factor = jnp.where(sub16 == 1, jnp.exp(t[0:1] - top), 1.0)
            total = t * factor if total is None else total + t * factor
        return jnp.where(sub16 == 0, top, total)

    got(R1.at[pl.ds(0, 7)], r_1)
    got(R1.at[pl.ds(0, 7)], s_1)
    total = merge([R1[k] for k in range(8)])
    mine = total
    for k in range(1, 4):
        mine = jnp.where(b == k, pltpu.roll(total, 128 - PROWS * k, 1), mine)
    lane4 = lax.broadcasted_iota(jnp.int32, (4, 128), 1) // PROWS
    packed = jnp.zeros((4, 128), F32)
    for k in range(4):
        rows = jnp.concatenate([mine[4 * r + k : 4 * r + k + 1] for r in range(4)], axis=0)
        packed = jnp.where(lane4 == k, pltpu.roll(rows, PROWS * k, 1) if k else rows, packed)
    S[y * 8 + z] = packed
    spread_far(S, y * 8 + z, 1, r_s, s_s)

    l_kc.wait()
    l_vc.wait()

    got(RO, r_so)
    for q in range(3):
        got(CR.at[part(q)], r_cr.at[q])
    reward0 = attend(0)
    for q in range(3, PARTS):
        got(CR.at[part(q)], r_cr.at[q])
    got(CR2, r_cr2)
    reward1 = attend(1)
    me = g * 32 + y * 8 + z
    Q[me] = jnp.concatenate([reward0, reward1], axis=0)
    spread_far(Q, me, 2, r_q, s_q)

    for cp in sends:
        cp.wait_send()
    others = pl.ds(0, 31)
    got(S.at[others], r_s)
    first = S[:, 0, :]
    lane1 = lax.broadcasted_iota(jnp.int32, (1, 128), 1) // PROWS
    lane32 = lax.broadcasted_iota(jnp.int32, (32, 128), 1) // PROWS
    top = jnp.max(first, axis=0, keepdims=True)
    factor = pltpu.roll(jnp.exp(first - top), PROWS, 1)
    first = jnp.sum(jnp.where(lane32 == 1, first * factor, first), axis=0, keepdims=True)
    total = jnp.sum(S[...], axis=0)
    total = jnp.concatenate([first, total[1:]], axis=0)
    log_total = pltpu.roll(jnp.log(jnp.where(lane1 == 1, first, 1.0)), 128 - PROWS, 1)

    def over_lanes(v):
        v = jnp.where(lane1 == 0, v, 0.0)
        return functools.reduce(jnp.add, [pltpu.roll(v, PROWS * k, 1) if k else v for k in range(4)])

    total = total - over_lanes(top) - over_lanes(log_total)
    for k in range(CAND):
        r, k4 = (k + 2) // 4, (k + 2) % 4
        row = total[r : r + 1]
        out[k : k + 1, :] = pltpu.roll(row, 128 - PROWS * k4, 1) if k4 else row
    got(S.at[others], s_s)
    others = pl.ds(0, 63)
    got(Q.at[others], r_q)
    reward = jnp.sum(Q[...], axis=0)
    both = jnp.where(sub16 < 8, reward[0:1], reward[1:2])
    spread_out = jnp.zeros((16, 128), F32)
    for k in range(8):
        spread_out = jnp.where(sub16 % 8 == k, pltpu.roll(both, (128 - 16 * k) % 128, 1), spread_out)
    out[16:32, :] = spread_out + jnp.pad(PV[...], ((0, 0), (0, 128 - CAND)))
    got(Q.at[others], s_q)


def place(packed, lp_out, rw_out, x, sem):
    cp = pltpu.make_async_copy(packed, x, sem)
    cp.start()
    cp.wait()
    lp_out[...] = x[0:CAND, :PROWS]
    rw_out[...] = x[16:32, :CAND]


def on_device(
    pol_hidden, pol_gain, pol_head, cand_ids, ext_hidden, ext_gain, query_w, key_w, value_w,
    key_cache, value_cache, cache_len, score_head, prev_logprob,
):
    vm = pltpu.VMEM
    dma = pltpu.SemaphoreType.DMA
    packed = pl.pallas_call(
        kernel,
        out_shape=jax.ShapeDtypeStruct((32, 128), F32),
        in_specs=[pl.BlockSpec(memory_space=pl.ANY)] * 14,
        out_specs=pl.BlockSpec(memory_space=vm),
        scratch_shapes=[
            vm((EROWS, D), BF16),
            vm((1, D), F32),
            vm((PROWS, D), BF16),
            vm((1, D), F32),
            vm((D, VOC), BF16),
            vm((16, 128), jnp.int32),
            vm((SLICE, 3 * HD), BF16),
            vm((16, CTX, HD), BF16),
            vm((16, CTX, HD), BF16),
            vm((1, 16), jnp.int32),
            vm((1, HD), F32),
            vm((16, CAND), F32),
            vm((4, 4 * EROWS, CH), BF16),
            vm((4, EROWS, CH), BF16),
            vm((2, EROWS, CH), BF16),
            vm((4, 4 * PROWS, SLICE), BF16),
            vm((EROWS, 3 * HD), F32),
            vm((EROWS, 3 * HD), F32),
            vm((EROWS, 3 * HD), F32),
            vm((EROWS, 3 * HD), F32),
            vm((EROWS, 3 * HD), F32),
            vm((EROWS, 3 * HD), F32),
            vm((EROWS, 4 * HD), BF16),
            vm((EROWS, 4 * HD), BF16),
            vm((SIZES[LAST], 4 * HD), BF16),
            vm((SIZES[LAST], 4 * HD), BF16),
            vm((8, 16, 128), F32),
            vm((64, 2, 128), F32),
            vm((32, 4, 128), F32),
            dma((19,)),
            dma((128,)),
            dma((2, PARTS)),
            dma,
            dma((3, PARTS)),
            dma((3, PARTS)),
            dma,
            dma((2,)),
            dma((3, 2)),
            dma((4,)),
            dma,
            dma((PARTS,)),
            dma((PARTS,)),
            dma,
            dma,
            dma,
            dma,
            dma,
            dma,
            dma,
            pltpu.SemaphoreType.REGULAR,
            pltpu.SemaphoreType.REGULAR,
            pltpu.SemaphoreType.REGULAR,
        ],
        compiler_params=pltpu.CompilerParams(
            collective_id=0, has_side_effects=True, vmem_limit_bytes=62 << 20
        ),
        name="candidates",
    )(
        pol_hidden, pol_gain.reshape(1, D), pol_head, cand_ids.T, ext_hidden, ext_gain.reshape(1, D),
        query_w, key_w, value_w, key_cache, value_cache, cache_len.reshape(1, 16),
        score_head.reshape(1, HD), prev_logprob,
    )
    logprob, combined = pl.pallas_call(
        place,
        out_shape=(
            jax.ShapeDtypeStruct((CAND, PROWS), F32),
            jax.ShapeDtypeStruct((16, CAND), F32),
        ),
        in_specs=[pl.BlockSpec(memory_space=pl.ANY)],
        scratch_shapes=[vm((32, 128), F32), dma],
        compiler_params=pltpu.CompilerParams(vmem_limit_bytes=62 << 20),
        name="place",
    )(packed)
    return logprob.T, combined


def solution(mesh):
    placed = (
        P("batch", None),
        P(),
        P(None, ("group", "batch", "mp")),
        P(),
        P("batch", None),
        P(),
        P("batch", ("group", "mp")),
        P("batch", ("group", "mp")),
        P("batch", ("group", "mp")),
        P("batch", None, ("group", "mp")),
        P("batch", None, ("group", "mp")),
        P("batch"),
        P(("group", "mp")),
        P("batch", None),
    )
    return jax.shard_map(
        on_device,
        mesh=mesh,
        in_specs=placed,
        out_specs=(P("batch", None), P("batch", None)),
        check_vma=False,
    )
```

```python
import functools

import jax
import jax.numpy as jnp
from jax import lax
from jax.experimental import pallas as pl
from jax.experimental.pallas import tpu as pltpu
from jax.sharding import PartitionSpec as P

MESH = pl.DeviceIdType.MESH
F32 = jnp.float32
BF16 = jnp.bfloat16

D = 8192
HD = 128
CAND = 10
CTX = 256
EROWS = 160
HALF = 80
PROWS = 32
SLICE = 2048
CH = 512
VOC = 256
STARTS = (0, 16, 48, 80, 112, 144)
SIZES = (16, 32, 32, 32, 32, 16)
PARTS = 6
LAST = PARTS - 1
GROUPS = ((0, 1), (2,), (3,), (4,))


def part(q):
    return pl.ds(STARTS[q], SIZES[q])


def kernel(
    ph, pg, phead, ids, eh, eg, qw, kw, vw, kc, vc, clen, sh, prev,
    out,
    H, EG, PH, PG, PW, IDS, W, KC, VC, CL, SH, PV,
    XR, SB, OB, XP, ACC, SO, RO, ST, RT, CS, CB, CR, CB2, CR2, R1, Q, S, SV,
    lsem, ssem, r_pull, r_sib, r_y, r_z, r_psib, r_pp, r_pn, r_pf, r_so, r_st, r_cr, r_cr2,
    r_1, s_1, r_q, s_q, r_s, s_s, met2, met3, met4,
):
    g = lax.axis_index("group")
    b = lax.axis_index("batch")
    m = lax.axis_index("mp")
    y, z, h, c = m % 4, m // 4, b // 2, b % 2
    oh = 1 - h

    def dev(dg, dh, y_, z_, c_):
        return (dg, 2 * dh + c_, 4 * z_ + y_)

    sib = dev(g, h, y, z, 1 - c)
    opp = [dev(1 - g, oh, y, z, k) for k in range(2)]
    xp_same = dev(g, oh, y, z, c)
    xp_other = dev(g, oh, y, z, 1 - c)
    ydev = [dev(g, h, (y + k) % 4, z, c) for k in range(4)]
    gydev = [dev(1 - g, h, (y + k) % 4, z, c) for k in range(4)]
    zdev = [dev(g, h, y, (z + k) % 8, c) for k in range(8)]

    def load(src, dst, k):
        cp = pltpu.make_async_copy(src, dst, lsem.at[k])
        cp.start()
        return cp

    l_ph = load(ph, PH, 0)
    l_pg = load(pg, PG, 1)
    l_eg = load(eg, EG, 2)
    l_h = [load(eh.at[part(q)], H.at[part(q)], 3 + q) for q in range(PARTS)]

    near = [sib, *opp, gydev[0], ydev[1], ydev[3], zdev[1], zdev[7]]
    near2 = [*near, ydev[2], zdev[2], zdev[6]]
    planes = [*ydev[1:], *gydev]
    barrier = pltpu.get_barrier_semaphore()
    for other in near:
        pl.semaphore_signal(barrier, inc=1, device_id=other, device_id_type=MESH)

    sends = []

    def send(src, dst, rsem, target):
        cp = pltpu.make_async_remote_copy(
            src_ref=src, dst_ref=dst, send_sem=ssem.at[len(sends)], recv_sem=rsem,
            device_id=target, device_id_type=MESH,
        )
        cp.start()
        sends.append(cp)

    def got(region, rsem):
        pltpu.make_async_copy(region, region, rsem).wait()

    def row_scale(ref, rows):
        acc = jnp.zeros((16, 512), F32)
        for k in range(D // 512):
            v = ref[rows, pl.ds(512 * k, 512)].astype(F32)
            acc = acc + v * v
        mean = jnp.sum(acc, axis=1, keepdims=True) * (1.0 / D)
        return lax.rsqrt(mean + 1e-05)

    jj = y * (1 - c) + (z % 4) * c

    def norm_piece(ref, gain, rows, r, start, width):
        cols = pl.ds(pl.multiple_of(start, 128), width)
        return (ref[rows, cols].astype(F32) * r * gain[:, cols]).astype(BF16)

    def pol_norm(i, _):
        rows = pl.ds(pl.multiple_of(16 * i, 16), 16)
        own = pl.ds(pl.multiple_of(PROWS * b + 16 * i, 16), 16)
        r = row_scale(PH, rows)
        for j in range(4):
            for k in range(4):
                XP[j, own, pl.ds(CH * k, CH)] = norm_piece(PH, PG, rows, r, j * SLICE + k * CH, CH)
        return 0

    def xp_rows(block):
        return pl.ds(pl.multiple_of(PROWS * block, 16), PROWS)

    def xp_half(block, e):
        return pl.ds(pl.multiple_of(PROWS * block + 16 * e, 16), 16)

    def greet(sem, others):
        for other in others:
            pl.semaphore_signal(sem, inc=1, device_id=other, device_id_type=MESH)

    l_ph.wait()
    l_pg.wait()
    lax.fori_loop(0, 2, pol_norm, 0)
    pl.semaphore_wait(barrier, len(near))
    greet(met2, near)
    for e in range(2):
        piece = XP.at[jj, xp_half(b, e)]
        send(piece, piece, r_pp.at[e], dev(1 - g, oh, y, z, c))
    own_p = XP.at[:, xp_rows(b)]
    send(own_p, own_p, r_psib, sib)

    def ext_norm(i, _):
        rows = pl.ds(pl.multiple_of(16 * i, 16), 16)
        r = row_scale(H, rows)
        for k in range(2):
            OB[k, rows, :] = norm_piece(H, EG, rows, r, (2 * oh + k) * SLICE + jj * CH, CH)
        own = pl.ds(pl.multiple_of(EROWS * b + 16 * i, 16), 16)
        for j in range(4):
            SB[j, rows, :] = norm_piece(H, EG, rows, r, (2 * h + 1 - c) * SLICE + j * CH, CH)
            XR[j, own, :] = norm_piece(H, EG, rows, r, b * SLICE + j * CH, CH)
        return 0

    def xr_rows(block, q):
        return pl.ds(pl.multiple_of(EROWS * block + STARTS[q], 16), SIZES[q])

    def xr_block(block):
        return pl.ds(pl.multiple_of(EROWS * block, 16), EROWS)

    l_eg.wait()
    def pull(q):
        for k in range(2):
            send(OB.at[k, part(q)], XR.at[jj, xr_rows(b, q)], r_pull.at[c, q], opp[k])

    for q in range(PARTS):
        l_h[q].wait()
        lax.fori_loop(STARTS[q] // 16, (STARTS[q] + SIZES[q]) // 16, ext_norm, 0)
        if q < 2:
            pull(q)
    send(SB, XR.at[:, xr_block(b)], r_sib, sib)
    l_w = [load(w, W.at[:, pl.ds(HD * k, HD)], 9 + k) for k, w in enumerate((qw, kw, vw))]

    l_pw = load(phead, PW, 12)
    l_kc = load(kc, KC, 13)
    l_vc = load(vc, VC, 14)
    l_small = [
        load(ids, IDS.at[pl.ds(0, CAND)], 15), load(clen, CL, 16), load(sh, SH, 17), load(prev, PV, 18)
    ]

    def project(*pieces):
        total = None
        for j in range(4):
            x = [XR[j, rows, :] for rows in pieces]
            x = x[0] if len(x) == 1 else jnp.concatenate(x, axis=0)
            term = jnp.dot(x, W[pl.ds(CH * j, CH), :], preferred_element_type=F32)
            total = term if total is None else total + term
        return total

    for cp in l_w:
        cp.wait()
    got(XR.at[:, xr_block(2 * h + 1 - c)], r_sib)
    both = project(xr_block(2 * h + 1 - c), xr_block(b))
    SO[...] = both[:EROWS]
    send(SO, RO, r_so, sib)
    ACC[...] = both[EROWS:]

    pl.semaphore_wait(met2, len(near))
    greet(met3, near2)

    pol_src = 2 * oh + c
    adev = [
        dev(g, h, (y + k * (1 - c)) % 4, (z + k * c) % 8, c) for k in (1, 7, 2, 6)
    ]
    def pol_on(e):
        piece = XP.at[jj, xp_half(pol_src, e)]
        got(piece, r_pp.at[e])
        send(piece, piece, r_pn.at[2, e], adev[2 + e])
        send(piece, piece, r_pn.at[0, e], adev[0])
        send(piece, piece, r_pn.at[1, e], adev[1])
        if e == 1:
            piece = XP.at[jj, xp_rows(pol_src)]
            send(piece, piece, r_pf.at[0], sib)

    def pol_pass(k):
        j = (jj + (3, 1, 2)[k]) % 4
        for e in range(2):
            got(XP.at[j, xp_half(pol_src, e)], r_pn.at[k, e])
        piece = XP.at[j, xp_rows(pol_src)]
        send(piece, piece, r_pf.at[k + 1], sib)

    def pass_on(q):
        piece = XR.at[y, xr_rows(2 * oh, q)]
        got(piece, r_pull.at[0, q])
        for k in (2, 1, 3):
            send(piece, piece, r_y.at[k - 1, q], ydev[k])
        piece = XR.at[z % 4, xr_rows(2 * oh + 1, q)]
        got(piece, r_pull.at[1, q])
        send(piece, piece, r_z.at[2, q], zdev[2 if q % 2 == 0 else 6])
        send(piece, piece, r_z.at[0, q], zdev[1])
        send(piece, piece, r_z.at[1, q], zdev[7])

    def ready(*group):
        for q in group:
            for k in (1, 3, 2):
                got(XR.at[(y - k + 4) % 4, xr_rows(2 * oh, q)], r_y.at[k - 1, q])
            rows = xr_rows(2 * oh + 1, q)
            got(XR.at[(z + 7) % 4, rows], r_z.at[0, q])
            got(XR.at[(z + 1) % 4, rows], r_z.at[1, q])
            got(XR.at[(z + 2) % 4, rows], r_z.at[2, q])
        size = sum(SIZES[q] for q in group)

        def rows_of(block):
            return pl.ds(pl.multiple_of(EROWS * block + STARTS[group[0]], 16), size)

        both = project(rows_of(2 * oh + 1 - c), rows_of(2 * oh + c))
        return both[:size], both[size:]

    def rows_in(n):
        return pl.ds(STARTS[GROUPS[n][0]], sum(SIZES[q] for q in GROUPS[n]))

    def exchange(n):
        theirs, ours = ready(*GROUPS[n])
        ST[rows_in(n), :] = theirs
        send(ST.at[rows_in(n)], RT.at[rows_in(n)], r_st.at[n], sib)
        CS[rows_in(n), :] = ours

    def split(ref, rows, total):
        query = total[:, :HD]
        high = query.astype(BF16)
        ref[rows, 0:HD] = high
        ref[rows, HD : 2 * HD] = (query - high.astype(F32)).astype(BF16)
        ref[rows, 2 * HD :] = total[:, HD:].astype(BF16)

    def cross(n):
        got(RT.at[rows_in(n)], r_st.at[n])
        split(CB, rows_in(n), CS[rows_in(n), :] + RT[rows_in(n), :])
        send(CB.at[rows_in(n)], CR.at[rows_in(n)], r_cr.at[n], xp_same)

    def cross_last():
        theirs, ours = ready(LAST)
        whole = pl.ds(0, SIZES[LAST])
        split(CB2, whole, theirs)
        send(CB2, CR2, r_cr2, xp_other)
        split(CB, part(LAST), ours)
        send(CB.at[part(LAST)], CR.at[part(LAST)], r_cr.at[4], xp_same)

    for cp in l_small:
        cp.wait()

    scale = 1.0 / HD**0.5
    slot = lax.broadcasted_iota(jnp.int32, (128, HALF), 0)
    src = lax.broadcasted_iota(jnp.int32, (128, HALF), 1)
    spread = jnp.where((src == (slot // 16) * CAND + slot % 16) & (slot % 16 < CAND), 1.0, 0.0).astype(BF16)
    r128 = lax.broadcasted_iota(jnp.int32, (128, 128), 0)
    l128 = lax.broadcasted_iota(jnp.int32, (128, 128), 1)
    position = lax.broadcasted_iota(jnp.int32, (128, CTX), 1)
    lens = jnp.pad(CL[...], ((0, 0), (0, 112)))

    def attend(s):
        mine = pl.ds(HALF * s, HALF)
        got_rows = CR[mine, :].astype(F32)
        if s == 1:
            tail = CR2[...].astype(F32)
            got_rows = got_rows + jnp.concatenate([jnp.zeros((HALF - SIZES[LAST], 4 * HD), F32), tail], axis=0)
        got_rows = jnp.concatenate(
            [got_rows[:, :HD] + got_rows[:, HD : 2 * HD], got_rows[:, 2 * HD :]], axis=1
        )
        qkv = (ACC[mine, :] + RO[mine, :] + got_rows).astype(BF16)
        qkv = jnp.dot(spread, qkv, preferred_element_type=F32)
        query, key_new, value_new = qkv[:, :HD], qkv[:, HD : 2 * HD], qkv[:, 2 * HD :]
        own = jnp.sum(query * key_new, axis=1, keepdims=True) * scale
        q16 = query.astype(BF16)
        scores = jnp.concatenate(
            [
                lax.dot_general(
                    q16[16 * p : 16 * p + 16], KC[8 * s + p],
                    (((1,), (1,)), ((), ())), preferred_element_type=F32,
                )
                for p in range(8)
            ],
            axis=0,
        ) * scale
        length = jnp.sum(jnp.where(l128 == r128 // 16 + 8 * s, lens, 0), axis=1, keepdims=True)
        valid = position < length
        scores = jnp.where(valid, scores, -1e30)
        peak = jnp.maximum(jnp.max(scores, axis=1, keepdims=True), own)
        expo = jnp.where(valid, jnp.exp(scores - peak), 0.0)
        own_expo = jnp.exp(own - peak)
        whole = jnp.sum(expo, axis=1, keepdims=True) + own_expo
        weights = (expo / whole).astype(BF16)
        own_weight = (own_expo / whole).astype(BF16).astype(F32)
        scored = jnp.concatenate(
            [jnp.broadcast_to(SV[8 * s + p : 8 * s + p + 1, :], (16, CTX)) for p in range(8)], axis=0
        )
        total = jnp.sum(weights.astype(F32) * scored, axis=1, keepdims=True)
        total = total + own_weight * jnp.sum(value_new * SH[...], axis=1, keepdims=True)
        return jnp.sum(jnp.where(r128 == l128, total, 0.0), axis=0, keepdims=True)

    def spread_one(buf, slot, rsem, sem, target):
        pltpu.make_async_remote_copy(
            src_ref=buf.at[slot], dst_ref=buf.at[slot], send_sem=sem, recv_sem=rsem,
            device_id=target, device_id_type=MESH,
        ).start()

    def spread_far(buf, slot, groups, rsem, sem):
        def far(o):
            return -(o[0] + min(o[1], 4 - o[1]) + min(o[2], 8 - o[2]))

        offsets = [(i, j, k) for i in range(groups) for j in range(4) for k in range(8) if i or j or k]
        for i, j, k in sorted(offsets, key=far):
            spread_one(buf, slot, rsem, sem, dev((g + i) % 2, h, (y + j) % 4, (z + k) % 8, c))

    pol_on(0)
    pol_on(1)
    pull(2)
    pass_on(0)
    pull(3)
    pass_on(1)
    pull(4)
    pl.semaphore_wait(met3, len(near2))
    greet(met4, planes)
    l_vc.wait()
    sh0 = SH[...]
    sh1 = sh0.astype(BF16)
    rest = sh0 - sh1.astype(F32)
    sh2 = rest.astype(BF16)
    sh3 = (rest - sh2.astype(F32)).astype(BF16)
    terms = jnp.concatenate([sh1, sh2, sh3, jnp.zeros((13, HD), BF16)], axis=0)
    for p in range(16):
        product = lax.dot_general(terms, VC[p], (((1,), (1,)), ((), ())), preferred_element_type=F32)
        SV[p : p + 1, :] = product[0:1] + product[1:2] + product[2:3]
    pass_on(2)
    pull(5)
    pol_pass(0)
    pol_pass(1)
    pass_on(3)
    exchange(0)
    pol_pass(2)
    pass_on(4)
    pass_on(5)
    got(XP.at[:, xp_rows(2 * h + 1 - c)], r_psib)
    sib_jj = y * c + (z % 4) * (1 - c)
    for k, shift in enumerate((0, 3, 1, 2)):
        got(XP.at[(sib_jj + shift) % 4, xp_rows(2 * oh + 1 - c)], r_pf.at[k])
    l_pw.wait()
    logits = None
    for j in range(4):
        term = jnp.dot(XP[j], PW[pl.ds(SLICE * j, SLICE), :], preferred_element_type=F32)
        logits = term if logits is None else logits + term

    exchange(1)
    cross(0)
    first_col = ((g * 4 + b) * 32 + m) * VOC
    logits = logits.T
    column = lax.broadcasted_iota(jnp.int32, (VOC, 128), 0) + first_col
    wanted = IDS[...]
    peak = jnp.max(logits, axis=0, keepdims=True)
    stats = [peak, jnp.sum(jnp.exp(logits - peak), axis=0, keepdims=True)]
    for k in range(CAND):
        stats.append(jnp.sum(jnp.where(column == wanted[k : k + 1, :], logits, 0.0), axis=0, keepdims=True))
    here = 2 * (2 * h + g) + c
    R1[here] = jnp.concatenate([*stats, jnp.zeros((4, 128), F32)], axis=0)
    for i, j, k in ((1, 0, 0), (1, 0, 1), (1, 1, 0), (1, 1, 1), (0, 1, 0), (0, 1, 1), (0, 0, 1)):
        spread_one(R1, here, r_1, s_1, dev((g + j) % 2, (h + i) % 2, y, z, (c + k) % 2))

    exchange(2)
    cross(1)
    exchange(3)
    cross(2)
    cross_last()
    cross(3)
    pl.semaphore_wait(met4, len(planes))

    sub16 = lax.broadcasted_iota(jnp.int32, (16, 128), 0)

    def merge(parts):
        top = functools.reduce(jnp.maximum, [t[0:1] for t in parts])
        total = None
        for t in parts:
            factor = jnp.where(sub16 == 1, jnp.exp(t[0:1] - top), 1.0)
            total = t * factor if total is None else total + t * factor
        return jnp.where(sub16 == 0, top, total)

    got(R1.at[pl.ds(0, 7)], r_1)
    got(R1.at[pl.ds(0, 7)], s_1)
    total = merge([R1[k] for k in range(8)])
    mine = total
    for k in range(1, 4):
        mine = jnp.where(b == k, pltpu.roll(total, 128 - PROWS * k, 1), mine)
    lane4 = lax.broadcasted_iota(jnp.int32, (4, 128), 1) // PROWS
    packed = jnp.zeros((4, 128), F32)
    for k in range(4):
        rows = jnp.concatenate([mine[4 * r + k : 4 * r + k + 1] for r in range(4)], axis=0)
        packed = jnp.where(lane4 == k, pltpu.roll(rows, PROWS * k, 1) if k else rows, packed)
    S[y * 8 + z] = packed
    spread_far(S, y * 8 + z, 1, r_s, s_s)

    l_kc.wait()

    got(RO, r_so)
    for n in range(2):
        got(CR.at[rows_in(n)], r_cr.at[n])
    reward0 = attend(0)
    for n in range(2, 4):
        got(CR.at[rows_in(n)], r_cr.at[n])
    got(CR.at[part(LAST)], r_cr.at[4])
    got(CR2, r_cr2)
    reward1 = attend(1)
    me = g * 32 + y * 8 + z
    Q[me] = jnp.concatenate([reward0, reward1], axis=0)
    spread_far(Q, me, 2, r_q, s_q)

    for cp in sends:
        cp.wait_send()
    others = pl.ds(0, 31)
    got(S.at[others], r_s)
    first = S[:, 0, :]
    lane1 = lax.broadcasted_iota(jnp.int32, (1, 128), 1) // PROWS
    lane32 = lax.broadcasted_iota(jnp.int32, (32, 128), 1) // PROWS
    top = jnp.max(first, axis=0, keepdims=True)
    factor = pltpu.roll(jnp.exp(first - top), PROWS, 1)
    first = jnp.sum(jnp.where(lane32 == 1, first * factor, first), axis=0, keepdims=True)
    total = jnp.sum(S[...], axis=0)
    total = jnp.concatenate([first, total[1:]], axis=0)
    log_total = pltpu.roll(jnp.log(jnp.where(lane1 == 1, first, 1.0)), 128 - PROWS, 1)

    def over_lanes(v):
        v = jnp.where(lane1 == 0, v, 0.0)
        return functools.reduce(jnp.add, [pltpu.roll(v, PROWS * k, 1) if k else v for k in range(4)])

    total = total - over_lanes(top) - over_lanes(log_total)
    for k in range(CAND):
        r, k4 = (k + 2) // 4, (k + 2) % 4
        row = total[r : r + 1]
        out[k : k + 1, :] = pltpu.roll(row, 128 - PROWS * k4, 1) if k4 else row
    got(S.at[others], s_s)
    others = pl.ds(0, 63)
    got(Q.at[others], r_q)
    reward = jnp.sum(Q[...], axis=0)
    both = jnp.where(sub16 < 8, reward[0:1], reward[1:2])
    spread_out = jnp.zeros((16, 128), F32)
    for k in range(8):
        spread_out = jnp.where(sub16 % 8 == k, pltpu.roll(both, (128 - 16 * k) % 128, 1), spread_out)
    out[16:32, :] = spread_out + jnp.pad(PV[...], ((0, 0), (0, 128 - CAND)))
    got(Q.at[others], s_q)


def place(packed, lp_out, rw_out, x, sem):
    cp = pltpu.make_async_copy(packed, x, sem)
    cp.start()
    cp.wait()
    lp_out[...] = x[0:CAND, :PROWS]
    rw_out[...] = x[16:32, :CAND]


def on_device(
    pol_hidden, pol_gain, pol_head, cand_ids, ext_hidden, ext_gain, query_w, key_w, value_w,
    key_cache, value_cache, cache_len, score_head, prev_logprob,
):
    vm = pltpu.VMEM
    dma = pltpu.SemaphoreType.DMA
    packed = pl.pallas_call(
        kernel,
        out_shape=jax.ShapeDtypeStruct((32, 128), F32),
        in_specs=[pl.BlockSpec(memory_space=pl.ANY)] * 14,
        out_specs=pl.BlockSpec(memory_space=vm),
        scratch_shapes=[
            vm((EROWS, D), BF16),
            vm((1, D), F32),
            vm((PROWS, D), BF16),
            vm((1, D), F32),
            vm((D, VOC), BF16),
            vm((16, 128), jnp.int32),
            vm((SLICE, 3 * HD), BF16),
            vm((16, CTX, HD), BF16),
            vm((16, CTX, HD), BF16),
            vm((1, 16), jnp.int32),
            vm((1, HD), F32),
            vm((16, CAND), F32),
            vm((4, 4 * EROWS, CH), BF16),
            vm((4, EROWS, CH), BF16),
            vm((2, EROWS, CH), BF16),
            vm((4, 4 * PROWS, SLICE), BF16),
            vm((EROWS, 3 * HD), F32),
            vm((EROWS, 3 * HD), F32),
            vm((EROWS, 3 * HD), F32),
            vm((EROWS, 3 * HD), F32),
            vm((EROWS, 3 * HD), F32),
            vm((EROWS, 3 * HD), F32),
            vm((EROWS, 4 * HD), BF16),
            vm((EROWS, 4 * HD), BF16),
            vm((SIZES[LAST], 4 * HD), BF16),
            vm((SIZES[LAST], 4 * HD), BF16),
            vm((8, 16, 128), F32),
            vm((64, 2, 128), F32),
            vm((32, 4, 128), F32),
            vm((16, CTX), F32),
            dma((19,)),
            dma((128,)),
            dma((2, PARTS)),
            dma,
            dma((3, PARTS)),
            dma((3, PARTS)),
            dma,
            dma((2,)),
            dma((3, 2)),
            dma((4,)),
            dma,
            dma((4,)),
            dma((5,)),
            dma,
            dma,
            dma,
            dma,
            dma,
            dma,
            dma,
            pltpu.SemaphoreType.REGULAR,
            pltpu.SemaphoreType.REGULAR,
            pltpu.SemaphoreType.REGULAR,
        ],
        compiler_params=pltpu.CompilerParams(
            collective_id=0, has_side_effects=True, vmem_limit_bytes=62 << 20
        ),
        name="candidates",
    )(
        pol_hidden, pol_gain.reshape(1, D), pol_head, cand_ids.T, ext_hidden, ext_gain.reshape(1, D),
        query_w, key_w, value_w, key_cache, value_cache, cache_len.reshape(1, 16),
        score_head.reshape(1, HD), prev_logprob,
    )
    logprob, combined = pl.pallas_call(
        place,
        out_shape=(
            jax.ShapeDtypeStruct((CAND, PROWS), F32),
            jax.ShapeDtypeStruct((16, CAND), F32),
        ),
        in_specs=[pl.BlockSpec(memory_space=pl.ANY)],
        scratch_shapes=[vm((32, 128), F32), dma],
        compiler_params=pltpu.CompilerParams(vmem_limit_bytes=62 << 20),
        name="place",
    )(packed)
    return logprob.T, combined


def solution(mesh):
    placed = (
        P("batch", None),
        P(),
        P(None, ("group", "batch", "mp")),
        P(),
        P("batch", None),
        P(),
        P("batch", ("group", "mp")),
        P("batch", ("group", "mp")),
        P("batch", ("group", "mp")),
        P("batch", None, ("group", "mp")),
        P("batch", None, ("group", "mp")),
        P("batch"),
        P(("group", "mp")),
        P("batch", None),
    )
    return jax.shard_map(
        on_device,
        mesh=mesh,
        in_specs=placed,
        out_specs=(P("batch", None), P("batch", None)),
        check_vma=False,
    )
```

```python
import functools

import jax
import jax.numpy as jnp
from jax import lax
from jax.experimental import pallas as pl
from jax.experimental.pallas import tpu as pltpu
from jax.sharding import PartitionSpec as P

MESH = pl.DeviceIdType.MESH
F32 = jnp.float32
BF16 = jnp.bfloat16

D = 8192
HD = 128
CAND = 10
CTX = 256
EROWS = 160
HALF = 80
PROWS = 32
SLICE = 2048
CH = 512
VOC = 256
STARTS = (0, 16, 48, 80, 112, 144)
SIZES = (16, 32, 32, 32, 32, 16)
PARTS = 6
LAST = PARTS - 1
GROUPS = ((0, 1), (2,), (3,), (4,))


def part(q):
    return pl.ds(STARTS[q], SIZES[q])


def kernel(
    ph, pg, phead, ids, eh, eg, qw, kw, vw, kc, vc, clen, sh, prev,
    out,
    H, EG, PH, PG, PW, IDS, W, KC, VC, CL, SH, PV,
    XR, SB, OB, XP, ACC, SO, RO, ST, RT, CS, CB, CR, CB2, CR2, R1, Q, S, SV,
    lsem, ssem, r_pull, r_sib, r_y, r_z, r_psib, r_pp, r_pn, r_pf, r_so, r_st, r_cr, r_cr2,
    r_1, s_1, r_q, s_q, r_s, s_s, met2, met3, met4,
):
    g = lax.axis_index("group")
    b = lax.axis_index("batch")
    m = lax.axis_index("mp")
    y, z, h, c = m % 4, m // 4, b // 2, b % 2
    oh = 1 - h

    def dev(dg, dh, y_, z_, c_):
        return (dg, 2 * dh + c_, 4 * z_ + y_)

    sib = dev(g, h, y, z, 1 - c)
    opp = [dev(1 - g, oh, y, z, k) for k in range(2)]
    xp_same = dev(g, oh, y, z, c)
    xp_other = dev(g, oh, y, z, 1 - c)
    ydev = [dev(g, h, (y + k) % 4, z, c) for k in range(4)]
    gydev = [dev(1 - g, h, (y + k) % 4, z, c) for k in range(4)]
    zdev = [dev(g, h, y, (z + k) % 8, c) for k in range(8)]

    def load(src, dst, k):
        cp = pltpu.make_async_copy(src, dst, lsem.at[k])
        cp.start()
        return cp

    l_ph = load(ph, PH, 0)
    l_pg = load(pg, PG, 1)
    l_eg = load(eg, EG, 2)
    l_h = [load(eh.at[part(q)], H.at[part(q)], 3 + q) for q in range(PARTS)]

    near = [sib, *opp, gydev[0], ydev[1], ydev[3], zdev[1], zdev[7]]
    near2 = [*near, ydev[2], zdev[2], zdev[6]]
    planes = [*ydev[1:], *gydev]
    barrier = pltpu.get_barrier_semaphore()
    for other in near:
        pl.semaphore_signal(barrier, inc=1, device_id=other, device_id_type=MESH)

    sends = []

    def send(src, dst, rsem, target):
        cp = pltpu.make_async_remote_copy(
            src_ref=src, dst_ref=dst, send_sem=ssem.at[len(sends)], recv_sem=rsem,
            device_id=target, device_id_type=MESH,
        )
        cp.start()
        sends.append(cp)

    def got(region, rsem):
        pltpu.make_async_copy(region, region, rsem).wait()

    def row_scale(ref, rows):
        acc = jnp.zeros((16, 512), F32)
        for k in range(D // 512):
            v = ref[rows, pl.ds(512 * k, 512)].astype(F32)
            acc = acc + v * v
        mean = jnp.sum(acc, axis=1, keepdims=True) * (1.0 / D)
        return lax.rsqrt(mean + 1e-05)

    jj = y * (1 - c) + (z % 4) * c

    def norm_piece(ref, gain, rows, r, start, width):
        cols = pl.ds(pl.multiple_of(start, 128), width)
        return (ref[rows, cols].astype(F32) * r * gain[:, cols]).astype(BF16)

    def pol_norm(i, _):
        rows = pl.ds(pl.multiple_of(16 * i, 16), 16)
        own = pl.ds(pl.multiple_of(PROWS * b + 16 * i, 16), 16)
        r = row_scale(PH, rows)
        for j in range(4):
            for k in range(4):
                XP[j, own, pl.ds(CH * k, CH)] = norm_piece(PH, PG, rows, r, j * SLICE + k * CH, CH)
        return 0

    def xp_rows(block):
        return pl.ds(pl.multiple_of(PROWS * block, 16), PROWS)

    def xp_half(block, e):
        return pl.ds(pl.multiple_of(PROWS * block + 16 * e, 16), 16)

    def greet(sem, others):
        for other in others:
            pl.semaphore_signal(sem, inc=1, device_id=other, device_id_type=MESH)

    l_ph.wait()
    l_pg.wait()
    lax.fori_loop(0, 2, pol_norm, 0)
    pl.semaphore_wait(barrier, len(near))
    greet(met2, near)
    for e in range(2):
        piece = XP.at[jj, xp_half(b, e)]
        send(piece, piece, r_pp.at[e], dev(1 - g, oh, y, z, c))
    own_p = XP.at[:, xp_rows(b)]
    send(own_p, own_p, r_psib, sib)

    def ext_norm(i, _):
        rows = pl.ds(pl.multiple_of(16 * i, 16), 16)
        r = row_scale(H, rows)
        for k in range(2):
            OB[k, rows, :] = norm_piece(H, EG, rows, r, (2 * oh + k) * SLICE + jj * CH, CH)
        own = pl.ds(pl.multiple_of(EROWS * b + 16 * i, 16), 16)
        for j in range(4):
            SB[j, rows, :] = norm_piece(H, EG, rows, r, (2 * h + 1 - c) * SLICE + j * CH, CH)
            XR[j, own, :] = norm_piece(H, EG, rows, r, b * SLICE + j * CH, CH)
        return 0

    def xr_rows(block, q):
        return pl.ds(pl.multiple_of(EROWS * block + STARTS[q], 16), SIZES[q])

    def xr_block(block):
        return pl.ds(pl.multiple_of(EROWS * block, 16), EROWS)

    l_eg.wait()
    def pull(q):
        for k in range(2):
            send(OB.at[k, part(q)], XR.at[jj, xr_rows(b, q)], r_pull.at[c, q], opp[k])

    for q in range(PARTS):
        l_h[q].wait()
        lax.fori_loop(STARTS[q] // 16, (STARTS[q] + SIZES[q]) // 16, ext_norm, 0)
        if q < 2:
            pull(q)
    send(SB, XR.at[:, xr_block(b)], r_sib, sib)
    l_w = [load(w, W.at[:, pl.ds(HD * k, HD)], 9 + k) for k, w in enumerate((qw, kw, vw))]

    l_pw = load(phead, PW, 12)
    l_kc = load(kc, KC, 13)
    l_vc = load(vc, VC, 14)
    l_small = [
        load(ids, IDS.at[pl.ds(0, CAND)], 15), load(clen, CL, 16), load(sh, SH, 17), load(prev, PV, 18)
    ]

    def project(*pieces):
        total = None
        for j in range(4):
            x = [XR[j, rows, :] for rows in pieces]
            x = x[0] if len(x) == 1 else jnp.concatenate(x, axis=0)
            term = jnp.dot(x, W[pl.ds(CH * j, CH), :], preferred_element_type=F32)
            total = term if total is None else total + term
        return total

    for cp in l_w:
        cp.wait()
    got(XR.at[:, xr_block(2 * h + 1 - c)], r_sib)
    both = project(xr_block(2 * h + 1 - c), xr_block(b))
    SO[...] = both[:EROWS]
    send(SO, RO, r_so, sib)
    ACC[...] = both[EROWS:]

    pl.semaphore_wait(met2, len(near))
    greet(met3, near2)

    pol_src = 2 * oh + c
    adev = [
        dev(g, h, (y + k * (1 - c)) % 4, (z + k * c) % 8, c) for k in (1, 7, 2, 6)
    ]
    def pol_on(e):
        piece = XP.at[jj, xp_half(pol_src, e)]
        got(piece, r_pp.at[e])
        send(piece, piece, r_pn.at[2, e], adev[2 + e])
        send(piece, piece, r_pn.at[0, e], adev[0])
        send(piece, piece, r_pn.at[1, e], adev[1])
        send(piece, piece, r_pf.at[0, e], sib)

    def pol_pass(k):
        j = (jj + (3, 1, 2)[k]) % 4
        for e in range(2):
            piece = XP.at[j, xp_half(pol_src, e)]
            got(piece, r_pn.at[k, e])
            send(piece, piece, r_pf.at[k + 1, e], sib)

    def pass_on(q):
        piece = XR.at[y, xr_rows(2 * oh, q)]
        got(piece, r_pull.at[0, q])
        for k in (2, 1, 3):
            send(piece, piece, r_y.at[k - 1, q], ydev[k])
        piece = XR.at[z % 4, xr_rows(2 * oh + 1, q)]
        got(piece, r_pull.at[1, q])
        send(piece, piece, r_z.at[2, q], zdev[2 if q % 2 == 0 else 6])
        send(piece, piece, r_z.at[0, q], zdev[1])
        send(piece, piece, r_z.at[1, q], zdev[7])

    def ready(*group):
        for q in group:
            for k in (1, 3, 2):
                got(XR.at[(y - k + 4) % 4, xr_rows(2 * oh, q)], r_y.at[k - 1, q])
            rows = xr_rows(2 * oh + 1, q)
            got(XR.at[(z + 7) % 4, rows], r_z.at[0, q])
            got(XR.at[(z + 1) % 4, rows], r_z.at[1, q])
            got(XR.at[(z + 2) % 4, rows], r_z.at[2, q])
        size = sum(SIZES[q] for q in group)

        def rows_of(block):
            return pl.ds(pl.multiple_of(EROWS * block + STARTS[group[0]], 16), size)

        both = project(rows_of(2 * oh + 1 - c), rows_of(2 * oh + c))
        return both[:size], both[size:]

    def rows_in(n):
        return pl.ds(STARTS[GROUPS[n][0]], sum(SIZES[q] for q in GROUPS[n]))

    def exchange(n):
        theirs, ours = ready(*GROUPS[n])
        ST[rows_in(n), :] = theirs
        send(ST.at[rows_in(n)], RT.at[rows_in(n)], r_st.at[n], sib)
        CS[rows_in(n), :] = ours

    def split(ref, rows, total):
        query = total[:, :HD]
        high = query.astype(BF16)
        ref[rows, 0:HD] = high
        ref[rows, HD : 2 * HD] = (query - high.astype(F32)).astype(BF16)
        ref[rows, 2 * HD :] = total[:, HD:].astype(BF16)

    def cross(n):
        got(RT.at[rows_in(n)], r_st.at[n])
        split(CB, rows_in(n), CS[rows_in(n), :] + RT[rows_in(n), :])
        send(CB.at[rows_in(n)], CR.at[rows_in(n)], r_cr.at[n], xp_same)

    def cross_last():
        theirs, ours = ready(LAST)
        whole = pl.ds(0, SIZES[LAST])
        split(CB2, whole, theirs)
        send(CB2, CR2, r_cr2, xp_other)
        split(CB, part(LAST), ours)
        send(CB.at[part(LAST)], CR.at[part(LAST)], r_cr.at[4], xp_same)

    for cp in l_small:
        cp.wait()

    scale = 1.0 / HD**0.5
    slot = lax.broadcasted_iota(jnp.int32, (128, HALF), 0)
    src = lax.broadcasted_iota(jnp.int32, (128, HALF), 1)
    spread = jnp.where((src == (slot // 16) * CAND + slot % 16) & (slot % 16 < CAND), 1.0, 0.0).astype(BF16)
    r128 = lax.broadcasted_iota(jnp.int32, (128, 128), 0)
    l128 = lax.broadcasted_iota(jnp.int32, (128, 128), 1)
    position = lax.broadcasted_iota(jnp.int32, (128, CTX), 1)
    lens = jnp.pad(CL[...], ((0, 0), (0, 112)))

    def attend(s):
        mine = pl.ds(HALF * s, HALF)
        got_rows = CR[mine, :].astype(F32)
        if s == 1:
            tail = CR2[...].astype(F32)
            got_rows = got_rows + jnp.concatenate([jnp.zeros((HALF - SIZES[LAST], 4 * HD), F32), tail], axis=0)
        got_rows = jnp.concatenate(
            [got_rows[:, :HD] + got_rows[:, HD : 2 * HD], got_rows[:, 2 * HD :]], axis=1
        )
        qkv = (ACC[mine, :] + RO[mine, :] + got_rows).astype(BF16)
        qkv = jnp.dot(spread, qkv, preferred_element_type=F32)
        query, key_new, value_new = qkv[:, :HD], qkv[:, HD : 2 * HD], qkv[:, 2 * HD :]
        own = jnp.sum(query * key_new, axis=1, keepdims=True) * scale
        q16 = query.astype(BF16)
        scores = jnp.concatenate(
            [
                lax.dot_general(
                    q16[16 * p : 16 * p + 16], KC[8 * s + p],
                    (((1,), (1,)), ((), ())), preferred_element_type=F32,
                )
                for p in range(8)
            ],
            axis=0,
        ) * scale
        length = jnp.sum(jnp.where(l128 == r128 // 16 + 8 * s, lens, 0), axis=1, keepdims=True)
        valid = position < length
        scores = jnp.where(valid, scores, -1e30)
        peak = jnp.maximum(jnp.max(scores, axis=1, keepdims=True), own)
        expo = jnp.where(valid, jnp.exp(scores - peak), 0.0)
        own_expo = jnp.exp(own - peak)
        whole = jnp.sum(expo, axis=1, keepdims=True) + own_expo
        weights = (expo / whole).astype(BF16)
        own_weight = (own_expo / whole).astype(BF16).astype(F32)
        scored = jnp.concatenate(
            [jnp.broadcast_to(SV[8 * s + p : 8 * s + p + 1, :], (16, CTX)) for p in range(8)], axis=0
        )
        total = jnp.sum(weights.astype(F32) * scored, axis=1, keepdims=True)
        total = total + own_weight * jnp.sum(value_new * SH[...], axis=1, keepdims=True)
        return jnp.sum(jnp.where(r128 == l128, total, 0.0), axis=0, keepdims=True)

    def spread_one(buf, slot, rsem, sem, target):
        pltpu.make_async_remote_copy(
            src_ref=buf.at[slot], dst_ref=buf.at[slot], send_sem=sem, recv_sem=rsem,
            device_id=target, device_id_type=MESH,
        ).start()

    def spread_far(buf, slot, groups, rsem, sem):
        def far(o):
            return -(o[0] + min(o[1], 4 - o[1]) + min(o[2], 8 - o[2]))

        offsets = [(i, j, k) for i in range(groups) for j in range(4) for k in range(8) if i or j or k]
        for i, j, k in sorted(offsets, key=far):
            spread_one(buf, slot, rsem, sem, dev((g + i) % 2, h, (y + j) % 4, (z + k) % 8, c))

    pol_on(0)
    pol_on(1)
    pull(2)
    pass_on(0)
    pull(3)
    pass_on(1)
    pull(4)
    pl.semaphore_wait(met3, len(near2))
    greet(met4, planes)
    l_vc.wait()
    sh0 = SH[...]
    sh1 = sh0.astype(BF16)
    rest = sh0 - sh1.astype(F32)
    sh2 = rest.astype(BF16)
    sh3 = (rest - sh2.astype(F32)).astype(BF16)
    terms = jnp.concatenate([sh1, sh2, sh3, jnp.zeros((13, HD), BF16)], axis=0)
    for p in range(16):
        product = lax.dot_general(terms, VC[p], (((1,), (1,)), ((), ())), preferred_element_type=F32)
        SV[p : p + 1, :] = product[0:1] + product[1:2] + product[2:3]
    pass_on(2)
    pull(5)
    pol_pass(0)
    pol_pass(1)
    pass_on(3)
    exchange(0)
    pol_pass(2)
    pass_on(4)
    pass_on(5)
    got(XP.at[:, xp_rows(2 * h + 1 - c)], r_psib)
    sib_jj = y * c + (z % 4) * (1 - c)
    for k, shift in enumerate((0, 3, 1, 2)):
        for e in range(2):
            got(XP.at[(sib_jj + shift) % 4, xp_half(2 * oh + 1 - c, e)], r_pf.at[k, e])
    l_pw.wait()
    logits = None
    for j in range(4):
        term = jnp.dot(XP[j], PW[pl.ds(SLICE * j, SLICE), :], preferred_element_type=F32)
        logits = term if logits is None else logits + term

    exchange(1)
    cross(0)
    first_col = ((g * 4 + b) * 32 + m) * VOC
    logits = logits.T
    column = lax.broadcasted_iota(jnp.int32, (VOC, 128), 0) + first_col
    wanted = IDS[...]
    peak = jnp.max(logits, axis=0, keepdims=True)
    stats = [peak, jnp.sum(jnp.exp(logits - peak), axis=0, keepdims=True)]
    for k in range(CAND):
        stats.append(jnp.sum(jnp.where(column == wanted[k : k + 1, :], logits, 0.0), axis=0, keepdims=True))
    here = 2 * (2 * h + g) + c
    R1[here] = jnp.concatenate([*stats, jnp.zeros((4, 128), F32)], axis=0)
    for i, j, k in ((1, 0, 0), (1, 0, 1), (1, 1, 0), (1, 1, 1), (0, 1, 0), (0, 1, 1), (0, 0, 1)):
        spread_one(R1, here, r_1, s_1, dev((g + j) % 2, (h + i) % 2, y, z, (c + k) % 2))

    exchange(2)
    cross(1)
    exchange(3)
    cross(2)
    cross_last()
    cross(3)
    pl.semaphore_wait(met4, len(planes))

    sub16 = lax.broadcasted_iota(jnp.int32, (16, 128), 0)

    def merge(parts):
        top = functools.reduce(jnp.maximum, [t[0:1] for t in parts])
        total = None
        for t in parts:
            factor = jnp.where(sub16 == 1, jnp.exp(t[0:1] - top), 1.0)
            total = t * factor if total is None else total + t * factor
        return jnp.where(sub16 == 0, top, total)

    got(R1.at[pl.ds(0, 7)], r_1)
    got(R1.at[pl.ds(0, 7)], s_1)
    total = merge([R1[k] for k in range(8)])
    mine = total
    for k in range(1, 4):
        mine = jnp.where(b == k, pltpu.roll(total, 128 - PROWS * k, 1), mine)
    lane4 = lax.broadcasted_iota(jnp.int32, (4, 128), 1) // PROWS
    packed = jnp.zeros((4, 128), F32)
    for k in range(4):
        rows = jnp.concatenate([mine[4 * r + k : 4 * r + k + 1] for r in range(4)], axis=0)
        packed = jnp.where(lane4 == k, pltpu.roll(rows, PROWS * k, 1) if k else rows, packed)
    S[y * 8 + z] = packed
    spread_far(S, y * 8 + z, 1, r_s, s_s)

    l_kc.wait()

    got(RO, r_so)
    for n in range(2):
        got(CR.at[rows_in(n)], r_cr.at[n])
    reward0 = attend(0)
    for n in range(2, 4):
        got(CR.at[rows_in(n)], r_cr.at[n])
    got(CR.at[part(LAST)], r_cr.at[4])
    got(CR2, r_cr2)
    reward1 = attend(1)
    me = g * 32 + y * 8 + z
    Q[me] = jnp.concatenate([reward0, reward1], axis=0)
    spread_far(Q, me, 2, r_q, s_q)

    for cp in sends:
        cp.wait_send()
    others = pl.ds(0, 31)
    got(S.at[others], r_s)
    first = S[:, 0, :]
    lane1 = lax.broadcasted_iota(jnp.int32, (1, 128), 1) // PROWS
    lane32 = lax.broadcasted_iota(jnp.int32, (32, 128), 1) // PROWS
    top = jnp.max(first, axis=0, keepdims=True)
    factor = pltpu.roll(jnp.exp(first - top), PROWS, 1)
    first = jnp.sum(jnp.where(lane32 == 1, first * factor, first), axis=0, keepdims=True)
    total = jnp.sum(S[...], axis=0)
    total = jnp.concatenate([first, total[1:]], axis=0)
    log_total = pltpu.roll(jnp.log(jnp.where(lane1 == 1, first, 1.0)), 128 - PROWS, 1)

    def over_lanes(v):
        v = jnp.where(lane1 == 0, v, 0.0)
        return functools.reduce(jnp.add, [pltpu.roll(v, PROWS * k, 1) if k else v for k in range(4)])

    total = total - over_lanes(top) - over_lanes(log_total)
    for k in range(CAND):
        r, k4 = (k + 2) // 4, (k + 2) % 4
        row = total[r : r + 1]
        out[k : k + 1, :] = pltpu.roll(row, 128 - PROWS * k4, 1) if k4 else row
    got(S.at[others], s_s)
    others = pl.ds(0, 63)
    got(Q.at[others], r_q)
    reward = jnp.sum(Q[...], axis=0)
    both = jnp.where(sub16 < 8, reward[0:1], reward[1:2])
    spread_out = jnp.zeros((16, 128), F32)
    for k in range(8):
        spread_out = jnp.where(sub16 % 8 == k, pltpu.roll(both, (128 - 16 * k) % 128, 1), spread_out)
    out[16:32, :] = spread_out + jnp.pad(PV[...], ((0, 0), (0, 128 - CAND)))
    got(Q.at[others], s_q)


def place(packed, lp_out, rw_out, x, sem):
    cp = pltpu.make_async_copy(packed, x, sem)
    cp.start()
    cp.wait()
    lp_out[...] = x[0:CAND, :PROWS]
    rw_out[...] = x[16:32, :CAND]


def on_device(
    pol_hidden, pol_gain, pol_head, cand_ids, ext_hidden, ext_gain, query_w, key_w, value_w,
    key_cache, value_cache, cache_len, score_head, prev_logprob,
):
    vm = pltpu.VMEM
    dma = pltpu.SemaphoreType.DMA
    packed = pl.pallas_call(
        kernel,
        out_shape=jax.ShapeDtypeStruct((32, 128), F32),
        in_specs=[pl.BlockSpec(memory_space=pl.ANY)] * 14,
        out_specs=pl.BlockSpec(memory_space=vm),
        scratch_shapes=[
            vm((EROWS, D), BF16),
            vm((1, D), F32),
            vm((PROWS, D), BF16),
            vm((1, D), F32),
            vm((D, VOC), BF16),
            vm((16, 128), jnp.int32),
            vm((SLICE, 3 * HD), BF16),
            vm((16, CTX, HD), BF16),
            vm((16, CTX, HD), BF16),
            vm((1, 16), jnp.int32),
            vm((1, HD), F32),
            vm((16, CAND), F32),
            vm((4, 4 * EROWS, CH), BF16),
            vm((4, EROWS, CH), BF16),
            vm((2, EROWS, CH), BF16),
            vm((4, 4 * PROWS, SLICE), BF16),
            vm((EROWS, 3 * HD), F32),
            vm((EROWS, 3 * HD), F32),
            vm((EROWS, 3 * HD), F32),
            vm((EROWS, 3 * HD), F32),
            vm((EROWS, 3 * HD), F32),
            vm((EROWS, 3 * HD), F32),
            vm((EROWS, 4 * HD), BF16),
            vm((EROWS, 4 * HD), BF16),
            vm((SIZES[LAST], 4 * HD), BF16),
            vm((SIZES[LAST], 4 * HD), BF16),
            vm((8, 16, 128), F32),
            vm((64, 2, 128), F32),
            vm((32, 4, 128), F32),
            vm((16, CTX), F32),
            dma((19,)),
            dma((128,)),
            dma((2, PARTS)),
            dma,
            dma((3, PARTS)),
            dma((3, PARTS)),
            dma,
            dma((2,)),
            dma((3, 2)),
            dma((4, 2)),
            dma,
            dma((4,)),
            dma((5,)),
            dma,
            dma,
            dma,
            dma,
            dma,
            dma,
            dma,
            pltpu.SemaphoreType.REGULAR,
            pltpu.SemaphoreType.REGULAR,
            pltpu.SemaphoreType.REGULAR,
        ],
        compiler_params=pltpu.CompilerParams(
            collective_id=0, has_side_effects=True, vmem_limit_bytes=62 << 20
        ),
        name="candidates",
    )(
        pol_hidden, pol_gain.reshape(1, D), pol_head, cand_ids.T, ext_hidden, ext_gain.reshape(1, D),
        query_w, key_w, value_w, key_cache, value_cache, cache_len.reshape(1, 16),
        score_head.reshape(1, HD), prev_logprob,
    )
    logprob, combined = pl.pallas_call(
        place,
        out_shape=(
            jax.ShapeDtypeStruct((CAND, PROWS), F32),
            jax.ShapeDtypeStruct((16, CAND), F32),
        ),
        in_specs=[pl.BlockSpec(memory_space=pl.ANY)],
        scratch_shapes=[vm((32, 128), F32), dma],
        compiler_params=pltpu.CompilerParams(vmem_limit_bytes=62 << 20),
        name="place",
    )(packed)
    return logprob.T, combined


def solution(mesh):
    placed = (
        P("batch", None),
        P(),
        P(None, ("group", "batch", "mp")),
        P(),
        P("batch", None),
        P(),
        P("batch", ("group", "mp")),
        P("batch", ("group", "mp")),
        P("batch", ("group", "mp")),
        P("batch", None, ("group", "mp")),
        P("batch", None, ("group", "mp")),
        P("batch"),
        P(("group", "mp")),
        P("batch", None),
    )
    return jax.shard_map(
        on_device,
        mesh=mesh,
        in_specs=placed,
        out_specs=(P("batch", None), P("batch", None)),
        check_vma=False,
    )
```
